256 devices in a mesh: lat: 16 (over z, x_lo), lon: 16 (over x_hi, y, core).
Axes of the slice: x: 4 (x_hi: 2, x_lo: 2; x = x_hi * 2 + x_lo), y: 4, z: 8, core: 2. Of those that a mesh axis runs over, the one named last changes fastest.
Arguments:
- tokens: bfloat16 [4, 192, 192, 512], P(None, 'lat', 'lon'), may hold values from -6 to 6
- cotangent: bfloat16 [4, 96, 96, 1024], P(None, 'lat', 'lon'), may hold values from -6 to 6
- first_inward: bfloat16 [512, 1536], replicated, may hold values from -0.25 to 0.25
- first_outward: bfloat16 [512, 512], replicated, may hold values from -0.25 to 0.25
- merge_weight: bfloat16 [2048, 1024], P('lon'), may hold values from -0.125 to 0.125
- second_inward: bfloat16 [1024, 3072], replicated, may hold values from -0.1875 to 0.1875
- second_outward: bfloat16 [1024, 1024], replicated, may hold values from -0.1875 to 0.1875
Outputs:
- second_out: bfloat16 [4, 96, 96, 1024], P(None, 'lat', 'lon')
- token_grad: bfloat16 [4, 192, 192, 512], P(None, 'lat', 'lon')
The draws below stay inside these ranges and needn't reach their ends.
All inputs are finite; a program needn't handle non-finite values.
Results may differ from the reference program's by a relative error of at most 0.023.
Values may be sent and summed in bfloat16 or wider, within the bound.
A program may use at most 128 MiB of HBM per device.

```python
import jax
import jax.numpy as jnp
from jax import lax

C1 = 512
C2 = 1024
HEADS1 = 8
HEADS2 = 16
LEV = 4
NLAT = 192
NLON = 192
NLAT2 = 96
NLON2 = 96


def level_of(stream_key, dims, cuts, smallest, high):
    level, own = 1.0, jax.random.fold_in(stream_key, 6)
    for dim, parts in cuts:
        steps = jnp.exp(jax.random.uniform(jax.random.fold_in(own, dim), (parts,), jnp.float32, smallest / len(cuts), high / len(cuts)))
        level = level * jnp.repeat(steps, dims[dim] // parts).reshape([-1 if axis == dim else 1 for axis in range(len(dims))])
    return level


def normal_values(key, dims, deviation, reach, split=(), kind=jnp.bfloat16):
    values = jax.random.normal(key, dims, jnp.float32) * deviation
    if len(split) > 0:
        values = level_of(key, dims, split, -0.22, 0.18) * values
    return jnp.clip(values, min=-reach, max=reach).astype(kind)


def setup_inputs(seed: int = 0) -> dict:
    keys = jax.random.split(jax.random.key(seed), 8)
    tokens = normal_values(keys[0], (LEV, NLAT, NLON, C1), 1.0, 6.0, ((1, 16), (2, 16)))
    cotangent = normal_values(keys[1], (LEV, NLAT2, NLON2, C2), 1.0, 6.0, ((1, 16), (2, 16)))
    first_inward = normal_values(keys[2], (C1, 3 * C1), C1 ** -0.5, 0.25)
    first_outward = normal_values(keys[3], (C1, C1), C1 ** -0.5, 0.25)
    merge_weight = normal_values(keys[4], (4 * C1, C2), (4 * C1) ** -0.5, 0.125, ((0, 16),))
    second_inward = normal_values(keys[5], (C2, 3 * C2), C2 ** -0.5, 0.1875)
    second_outward = normal_values(keys[6], (C2, C2), C2 ** -0.5, 0.1875)
    return {"tokens": tokens, "cotangent": cotangent, "first_inward": first_inward, "first_outward": first_outward, "merge_weight": merge_weight, "second_inward": second_inward, "second_outward": second_outward}


eps_norm = 1e-05

def normalize(vector):
    center = vector - lax.optimization_barrier(jnp.mean(vector, axis=-1, keepdims=True))
    spread = lax.optimization_barrier(jnp.mean(center * center, axis=-1, keepdims=True))
    return center * lax.rsqrt(spread + eps_norm)

def to_windows(grid_field, span):
    levels, lat_cells, lon_cells, channels = grid_field.shape
    shaped = grid_field.reshape(levels // 2, 2, lat_cells // 6, 6, lon_cells // span, span, channels)
    return shaped.transpose(0, 2, 4, 1, 3, 5, 6).reshape(-1, 12 * span, channels)

def from_windows(blocks, levels, lat_cells, lon_cells, span):
    channels = blocks.shape[-1]
    shaped = blocks.reshape(levels // 2, lat_cells // 6, lon_cells // span, 2, 6, span, channels)
    return shaped.transpose(0, 3, 1, 4, 2, 5, 6).reshape(levels, lat_cells, lon_cells, channels)

def region_labels(levels, lat_cells, offset, lat_total):
    level_part = (jnp.arange(levels, dtype=jnp.int32) >= levels - 1).astype(jnp.int32)
    row_part = (offset + jnp.arange(lat_cells, dtype=jnp.int32) >= lat_total - 3).astype(jnp.int32)
    return level_part[:, None] * 2 + row_part[None, :]

def window_labels(labels, lon_cells, span):
    spread_out = jnp.broadcast_to(labels[:, :, None, None], labels.shape + (lon_cells, 1))
    return to_windows(spread_out, span)[:, :, 0]

def attend(queries, keys_in, values_in, query_labels, key_labels, head_count):
    number, query_len, channels = queries.shape
    key_len = keys_in.shape[1]
    head_size = channels // head_count
    query_heads = queries.astype(jnp.float32).reshape(number, query_len, head_count, head_size)
    key_heads = keys_in.astype(jnp.float32).reshape(number, key_len, head_count, head_size)
    value_heads = values_in.astype(jnp.float32).reshape(number, key_len, head_count, head_size)
    scores = jnp.einsum('nqhd,nkhd->nhqk', query_heads, key_heads) * head_size ** (-0.5)
    allowed = query_labels[:, None, :, None] == key_labels[:, None, None, :]
    raised = jnp.where(allowed, jnp.exp(scores), 0.0)
    shares = (raised / lax.optimization_barrier(jnp.sum(raised, axis=-1, keepdims=True))).astype(jnp.bfloat16)
    blended = jnp.einsum('nhqk,nkhd->nqhd', shares.astype(jnp.float32), value_heads)
    return blended.reshape(number, query_len, channels).astype(jnp.bfloat16)

def attend_grouped(queries, keys_in, values_in, labels, head_count):
    window_total = queries.shape[0]

    def one_group(members):
        return attend(members[0], members[1], members[2], members[3], members[3], head_count)
    grouped = tuple((member.reshape((8, window_total // 8) + member.shape[1:]) for member in (queries, keys_in, values_in, labels)))
    result = lax.map(jax.checkpoint(one_group), grouped)
    return result.reshape((window_total,) + result.shape[2:])

def window_section(grid_field, inward, outward, head_count):
    levels, lat_cells, lon_cells, channels = grid_field.shape
    blocks = to_windows(grid_field, 12)
    number = blocks.shape[0]
    triple = jnp.dot(blocks.reshape(-1, channels), inward, preferred_element_type=jnp.float32).astype(jnp.bfloat16)
    triple = triple.reshape(number, -1, 3 * channels)
    labels = window_labels(region_labels(levels, lat_cells, 0, lat_cells), lon_cells, 12)
    blended = attend_grouped(triple[..., :channels], triple[..., channels:2 * channels], triple[..., 2 * channels:], labels, head_count)
    projected = jnp.dot(blended.reshape(-1, channels), outward, preferred_element_type=jnp.float32).astype(jnp.bfloat16)
    return from_windows(projected.reshape(number, -1, channels), levels, lat_cells, lon_cells, 12)

def shifted(grid_field, direction):
    return jnp.roll(grid_field, (-direction, -3 * direction, -6 * direction), axis=(0, 1, 2))

def merge_patches(grid_field):
    levels, lat_cells, lon_cells, channels = grid_field.shape
    shaped = grid_field.reshape(levels, lat_cells // 2, 2, lon_cells // 2, 2, channels).transpose(0, 1, 3, 2, 4, 5)
    return shaped.reshape(levels, lat_cells // 2, lon_cells // 2, 4 * channels)

def forward(tokens, first_inward, first_outward, merge_weight, second_inward, second_outward):
    wide_tokens = tokens.astype(jnp.float32)
    normed = normalize(wide_tokens).astype(jnp.bfloat16)
    attended = shifted(window_section(shifted(normed, 1), first_inward, first_outward, HEADS1), -1)
    first_out = (wide_tokens + attended.astype(jnp.float32)).astype(jnp.bfloat16)
    merged = merge_patches(first_out)
    levels, lat_cells, lon_cells, channels = merged.shape
    merged_norm = normalize(merged.astype(jnp.float32)).astype(jnp.bfloat16)
    reduced = jnp.dot(merged_norm.reshape(-1, channels), merge_weight, preferred_element_type=jnp.float32).astype(jnp.bfloat16)
    reduced = reduced.reshape(levels, lat_cells, lon_cells, merge_weight.shape[1])
    reduced_wide = reduced.astype(jnp.float32)
    normed_two = normalize(reduced_wide).astype(jnp.bfloat16)
    attended_two = shifted(window_section(shifted(normed_two, 1), second_inward, second_outward, HEADS2), -1)
    return (reduced_wide + attended_two.astype(jnp.float32)).astype(jnp.bfloat16)

def reference(tokens, cotangent, first_inward, first_outward, merge_weight, second_inward, second_outward):

    def apply_all(grid_field):
        return forward(grid_field, first_inward, first_outward, merge_weight, second_inward, second_outward)
    output, pullback = jax.vjp(apply_all, tokens)
    return (output, pullback(cotangent)[0])
```

```python
import functools

import jax
import jax.numpy as jnp
import numpy as np
from jax import lax
from jax.experimental import pallas as pl
from jax.experimental.pallas import tpu as pltpu
from jax.sharding import PartitionSpec as P

F32 = jnp.float32
BF = jnp.bfloat16
NT = ((1,), (1,))
TN = ((0,), (0,))
EPS = 1e-05
MESH = pl.DeviceIdType.MESH


def dot(a, b, dims=((1,), (0,))):
    return lax.dot_general(a, b, (dims, ((), ())), preferred_element_type=F32)


def window_place(level, row_half, counters):
    key = ("a", row_half) if level in (1, 2) else (level, row_half)
    start = {("a", 0): 0, ("a", 1): 72, (3, 0): 144, (3, 1): 180, (0, 0): 216, (0, 1): 252}[key]
    taken = counters.get(key, 0)
    counters[key] = taken + 1
    return start + taken


@functools.lru_cache(None)
def orders():
    raw = np.zeros((144, 192), np.float32)
    for h in range(2):
        for slab in range(12):
            for k in range(6):
                raw[h * 72 + slab * 6 + k, slab * 16 + 6 * h + k] = 1
    one = np.zeros((288, 288), np.float32)
    counters = {}
    for h in range(2):
        for g in range(2):
            for lev in range(4):
                for k in range(18):
                    one[window_place(lev, g, counters), (h * 2 + g) * 72 + lev * 18 + k] = 1
    two = np.zeros((288, 288), np.float32)
    counters = {}
    for m in range(2):
        for h in range(2):
            for lev in range(4):
                for i in range(6):
                    for j in range(3):
                        two[window_place(lev, i // 3, counters), m * 144 + h * 72 + lev * 18 + i * 3 + j] = 1
    merge = np.zeros((288, 288), np.float32)
    for p in range(2):
        for q in range(2):
            for lev in range(4):
                for i in range(6):
                    for j in range(3):
                        row, col = 2 * i + p, 2 * j + q
                        source = (row // 3) * 72 + lev * 18 + (row % 3) * 6 + col
                        merge[(p * 2 + q) * 72 + lev * 18 + i * 3 + j, source] = 1
    coarse = np.zeros((144, 192), np.float32)
    for h in range(2):
        for lev in range(4):
            for i in range(6):
                for j in range(3):
                    slab = ((i // 3) * 4 + lev) * 3 + i % 3
                    coarse[h * 72 + lev * 18 + i * 3 + j, slab * 8 + h * 3 + j] = 1
    mats = (raw, one, one.T, two, two.T, merge, merge.T, coarse, coarse.T)
    return tuple(np.asarray(m, dtype=BF) for m in mats)


def head_rows():
    lane = lax.broadcasted_iota(jnp.int32, (1, 256), 1)
    return [jnp.where((lane >= 64 * h) & (lane < 64 * h + 64), 1.0, 0.0).astype(BF) for h in range(4)]


def stack(x, rows):
    pad = jnp.zeros((16, 256), BF)
    parts = []
    for r in rows:
        parts += [x * r, pad]
    return jnp.concatenate(parts, axis=0)


def unstack(y):
    lane = lax.broadcasted_iota(jnp.int32, (144, 256), 1)
    out = y[480:624]
    for h in (2, 1, 0):
        out = jnp.where(lane < 64 * h + 64, y[160 * h : 160 * h + 144], out)
    return out


def attend(trip, mask, mixed, shares):
    rows = head_rows()
    for s in range(2):
        for g in range(2):
            r = pl.ds(144 * s, 144)
            q = trip[r, pl.ds(256 * g, 256)] * jnp.asarray(0.125, BF)
            k = trip[r, pl.ds(512 + 256 * g, 256)]
            v = trip[r, pl.ds(1024 + 256 * g, 256)]
            raised = jnp.exp(dot(k, stack(q, rows), NT) + mask[s])
            p = (raised * (1.0 / jnp.sum(raised, axis=0, keepdims=True))).astype(BF)
            shares[2 * s + g] = p
            mixed[r, pl.ds(256 * g, 256)] = unstack(dot(p, v, TN)).astype(BF)


def attend_back(trip, grad_mixed, shares, grad_trip):
    rows = head_rows()
    for s in range(2):
        for g in range(2):
            r = pl.ds(144 * s, 144)
            q = trip[r, pl.ds(256 * g, 256)] * jnp.asarray(0.125, BF)
            k = trip[r, pl.ds(512 + 256 * g, 256)]
            v = trip[r, pl.ds(1024 + 256 * g, 256)]
            do = stack(grad_mixed[r, pl.ds(256 * g, 256)], rows)
            p = shares[2 * s + g]
            wide = p.astype(F32)
            t = wide * dot(v, do, NT)
            ds = (t - wide * jnp.sum(t, axis=0, keepdims=True)).astype(BF)
            grad_trip[r, pl.ds(1024 + 256 * g, 256)] = dot(p, do).astype(BF)
            grad_trip[r, pl.ds(512 + 256 * g, 256)] = dot(ds, stack(q, rows)).astype(BF)
            grad_trip[r, pl.ds(256 * g, 256)] = (unstack(dot(ds, k, TN)) * 0.125).astype(BF)


def norm(x):
    center = x - jnp.mean(x, axis=-1, keepdims=True)
    scale = lax.rsqrt(jnp.mean(center * center, axis=-1, keepdims=True) + EPS)
    return center * scale, scale


def norm_back(grad, hat, scale):
    first = jnp.mean(grad, axis=-1, keepdims=True)
    second = jnp.mean(grad * hat, axis=-1, keepdims=True)
    return scale * (grad - first - hat * second)


SCRATCH = dict(
    raw=((4, 12, 12, 512), BF),
    own=((2, 4, 72, 512), BF),
    tok=((2, 4, 72, 512), BF),
    nrm=((2, 288, 512), BF),
    rs1=((2, 288, 128), F32),
    trip1=((2, 288, 1536), BF),
    ps1=((2, 4, 144, 640), BF),
    mix=((288, 512), BF),
    mk=((2, 2, 144, 640), F32),
    fo=((2, 4, 72, 512), BF),
    lay=((2, 4, 72, 512), BF),
    mf=((144, 2048), F32),
    mn=((144, 2048), BF),
    rsm=((144, 128), F32),
    red=((144, 1024), BF),
    nt=((2, 144, 1024), BF),
    rs2=((144, 128), F32),
    w1i_v=((512, 1536), BF),
    w1o_v=((512, 512), BF),
    wmv=((16, 128, 1024), BF),
    w2i_v=((1024, 1536), BF),
    w2o_v=((1024, 1024), BF),
    c_raw=((144, 192), BF),
    one=((288, 288), BF),
    one_t=((288, 288), BF),
    two=((288, 288), BF),
    two_t=((288, 288), BF),
    mer=((288, 288), BF),
    mer_t=((288, 288), BF),
    coa=((144, 192), BF),
    coa_t=((192, 144), BF),
    cot_r=((2, 4, 3, 6, 1024), BF),
    cot2=((2, 144, 1024), BF),
    trip2=((288, 1536), BF),
    ps2=((4, 144, 640), BF),
    mix2=((288, 512), BF),
    mxo=((144, 512), BF),
    mxs=((144, 512), BF),
    mxr=((144, 512), BF),
    dmix=((288, 512), BF),
    dmix2=((288, 512), BF),
    dtrip=((288, 1536), BF),
    pgs=((144, 1024), BF),
    pgr=((144, 1024), BF),
    pgo=((144, 1024), F32),
    gr=((144, 1024), BF),
    gmn=((144, 2048), BF),
    gf=((2, 4, 72, 512), BF),
    g1=((2, 4, 72, 512), BF),
    tg=((2, 4, 72, 512), BF),
    s2o=((2, 4, 3, 6, 1024), BF),
)
N_IN = 16
N_SEM = 80


class Remote:
    def __init__(self, copy, when):
        self.copy, self.when = copy, when

    def run(self, act, when):
        if when is None:
            act()
        else:
            pl.when(when)(act)

    def start(self):
        self.run(self.copy.start, self.when)

    def wait_send(self):
        self.run(self.copy.wait_send, self.when)

    def wait_recv(self, when=None):
        self.run(self.copy.wait_recv, self.when if when is None else when)


class Copies:
    def __init__(self, local, send, recv):
        self.local_sems, self.send_sems, self.recv_sems = local, send, recv
        self.locals, self.remotes = 0, []

    def local(self, source, target):
        copy = pltpu.make_async_copy(source, target, self.local_sems.at[self.locals])
        self.locals += 1
        copy.start()
        return copy

    def send(self, source, target, device, when=None):
        place = len(self.remotes)
        copy = pltpu.make_async_remote_copy(
            src_ref=source,
            dst_ref=target,
            send_sem=self.send_sems.at[place],
            recv_sem=self.recv_sems.at[place],
            device_id=device,
            device_id_type=MESH,
        )
        remote = Remote(copy, when)
        remote.start()
        self.remotes.append(remote)
        return remote


class Gather:
    def __init__(self, net, wm, wmv, i, j, lats):
        self.net, self.wmv, self.i = net, wmv, i
        x_hi = j // 8
        y2 = j - x_hi * 8
        self.odd = lax.rem(i // 2, 2)
        across = i + 1 - 2 * lax.rem(i, 2)

        def same(k):
            return x_hi * 8 + lax.rem(y2 + 2 * k + 8, 8)

        def other(k):
            return (1 - x_hi) * 8 + lax.rem(y2 + 2 * k + 8, 8)

        def pick(when_odd, when_even):
            return when_odd * self.odd + when_even * (1 - self.odd)

        self.mate = (i, j + 1 - 2 * lax.rem(j, 2))
        self.z_up, self.z_down = (lax.rem(i + 2, lats), j), (lax.rem(i + lats - 2, lats), j)
        self.targets = [
            (pick(i, across), pick(same(-1), other(-1))),
            (pick(i, across), pick(same(1), other(1))),
            (pick(across, i), pick(other(0), same(2))),
            (across, other(2)),
        ]
        self.mine = [pick(same(1), other(1)), pick(same(-1), other(-1)), pick(other(0), same(2)), other(2)]
        self.theirs = [pick(other(1), same(1)), pick(other(-1), same(-1)), pick(same(2), other(0)), other(2)]
        self.partners = [self.z_up, self.z_down]
        for step in (-1, 1):
            self.partners += [(i, same(step)), (across, other(step))]
        self.partners += [(i, same(2)), (across, other(0)), (across, other(2))]
        self.direct, self.from_z, self.to_mate = {}, {}, []
        self.wm, self.j = wm, j

    def part(self, block, row, rows):
        return self.wmv.at[block, pl.ds(row, rows)]

    def when(self, slot, value):
        return None if slot < 3 else self.odd == value

    def start(self):
        for half in range(2):
            rows = pl.ds(64 * half, 64)
            for slot in range(4):
                self.direct[slot, half] = self.net.send(
                    self.wm.at[rows], self.wmv.at[self.j, rows], self.targets[slot], when=self.when(slot, 1)
                )
        self.to_mate.append(self.net.send(self.wm, self.wmv.at[self.j], self.mate))

    def forward(self, half):
        for slot in (2, 0, 1, 3):
            self.direct[slot, half].wait_recv()
            block, when = self.mine[slot], self.when(slot, 1)
            low, high = self.part(block, 64 * half, 32), self.part(block, 64 * half + 32, 32)
            self.from_z[slot, half] = (
                self.net.send(low, low, self.z_up, when=when),
                self.net.send(high, high, self.z_down, when=when),
            )
            if slot < 3:
                whole = self.part(block, 64 * half, 64)
                self.to_mate.append(self.net.send(whole, whole, self.mate))

    def swapped(self, half):
        for slot in (2, 0, 1, 3):
            for copy in self.from_z[slot, half]:
                copy.wait_recv(self.when(slot, 0))
            whole = self.part(self.theirs[slot], 64 * half, 64)
            self.to_mate.append(self.net.send(whole, whole, self.mate))

    def finish(self):
        for copy in self.to_mate:
            copy.wait_recv()


def body(lats, lons, *refs):
    (tok_in, cot_in, w1i, w1o, wm, w2i, w2o, c0, c1, c1t, c2, c2t, c3, c3t, c4, c4t) = refs[:N_IN]
    out2, outg = refs[N_IN : N_IN + 2]
    rest = refs[N_IN + 2 :]
    v = dict(zip(SCRATCH, rest))
    net = Copies(*rest[len(SCRATCH) :])
    own, tok, fo, lay, g1, gf, tg, wmv = (v[n] for n in ("own", "tok", "fo", "lay", "g1", "gf", "tg", "wmv"))

    i, j = lax.axis_index("lat"), lax.axis_index("lon")
    up, down = lax.rem(i + 1, lats), lax.rem(i + lats - 1, lats)
    right, left = lax.rem(j + 1, lons), lax.rem(j + lons - 1, lons)
    core = lax.rem(j, 2)
    mate = j + 1 - 2 * core
    ring = lons == 16
    partners = [(i, right), (i, left), (up, j), (down, j), (up, right), (down, left)]
    gather = Gather(net, wm, wmv, i, j, lats) if ring else None
    partners += gather.partners if ring else [(i, lax.rem(j + d, lons)) for d in range(1, lons)]

    barrier = pltpu.get_barrier_semaphore()
    for device in partners:
        pl.semaphore_signal(barrier, inc=1, device_id=device, device_id_type=MESH)

    in_raw = net.local(tok_in, v["raw"])
    in_c_raw = net.local(c0, v["c_raw"])
    in_one = net.local(c1, v["one"])
    in_w1i = net.local(w1i, v["w1i_v"])
    in_w1o = net.local(w1o, v["w1o_v"])
    in_one_t = net.local(c1t, v["one_t"])
    in_wm = net.local(wm, wmv.at[j])
    in_rest = [net.local(a, v[n]) for a, n in ((c4, "coa"), (c3, "mer"), (c2, "two"))]
    in_w2i = [
        net.local(
            w2i.at[:, pl.ds(pl.multiple_of(1024 * part + 512 * core, 512), 512)],
            v["w2i_v"].at[:, pl.ds(512 * part, 512)],
        )
        for part in range(3)
    ]
    in_w2o = net.local(w2o, v["w2o_v"])
    in_late = [net.local(a, v[n]) for a, n in ((c2t, "two_t"), (c3t, "mer_t"), (c4t, "coa_t"))]

    in_raw.wait()
    in_c_raw.wait()
    for g in range(4):
        slabs = []
        for lev in range(4):
            for r in range(3):
                slabs += [v["raw"][lev, 3 * g + r].astype(F32), jnp.zeros((4, 512), F32)]
        value = dot(v["c_raw"][...], jnp.concatenate(slabs, axis=0).astype(BF))
        for h in range(2):
            own[h, g] = value[72 * h : 72 * h + 72].astype(BF)

    pl.semaphore_wait(barrier, len(partners))

    r_a = net.send(own.at[0, pl.ds(1, 2)], tok.at[1, pl.ds(0, 2)], (i, left))
    r_b = net.send(own.at[0, pl.ds(3, 1)], tok.at[1, pl.ds(2, 1)], (i, left))
    r_c = net.send(own.at[1, pl.ds(0, 1)], tok.at[0, pl.ds(3, 1)], (down, j))
    r_d = net.send(own.at[0, pl.ds(0, 1)], tok.at[1, pl.ds(3, 1)], (down, left))

    depth = wm.shape[0]
    everywhere = []
    if ring:
        gather.start()
    else:
        for d in range(1, lons):
            everywhere.append(net.send(wm, wmv.at[j], (i, lax.rem(j + d, lons))))

    def merge_rows(b):
        if depth <= 256:
            count = 256 // depth
            return wmv[pl.ds(count * b, count)].reshape(256, 1024)
        return wmv[256 * b // depth, pl.ds(256 * b % depth, 256)]

    cot_a = net.send(cot_in.at[:, pl.ds(3, 3)], v["cot_r"].at[0], (i, left))
    cot_b = net.send(cot_in.at[:, pl.ds(0, 3)], v["cot_r"].at[1], (down, left))

    lane = lax.broadcasted_iota(jnp.int32, (1, 640), 1)
    lane = lane - 160 * (
        (lane >= 160).astype(jnp.int32) + (lane >= 320).astype(jnp.int32) + (lane >= 480).astype(jnp.int32)
    )
    key = lax.broadcasted_iota(jnp.int32, (144, 1), 0)

    def quarter(index):
        return (index >= 36).astype(jnp.int32) + (index >= 72).astype(jnp.int32) + (index >= 108).astype(jnp.int32)

    pad = lane >= 144
    half_mask = jnp.where(((key >= 72) == (lane >= 72)) | pad, 0.0, -1e30)
    quarter_mask = jnp.where((quarter(key) == quarter(lane)) | pad, 0.0, -1e30)
    last = jnp.broadcast_to(i, (144, 640)) == lats - 1
    v["mk"][0, 0] = jnp.zeros((144, 640), F32)
    v["mk"][0, 1] = half_mask
    v["mk"][1, 0] = jnp.where(last, half_mask, 0.0)
    v["mk"][1, 1] = jnp.where(last, quarter_mask, half_mask)

    def rows_of(parts):
        return jnp.concatenate([part.astype(F32) for part in parts], axis=0)

    def rolled(h, g):
        return own[1, g + 1] if h == 0 and g < 3 else tok[h, g]

    def rolled_tokens(w):
        return rows_of([rolled(h, 2 * w + g) for h in range(2) for g in range(2)])

    def put_pieces(ref, w, value):
        for k in range(4):
            ref[k // 2, 2 * w + k % 2] = value[72 * k : 72 * k + 72].astype(BF)

    def section_one(w):
        x = rolled_tokens(w)
        hat, scale = norm(x)
        normed = hat.astype(BF)
        v["nrm"][w] = normed
        v["rs1"][w] = jnp.broadcast_to(scale, (288, 128))
        blocks = dot(v["one"][...], normed).astype(BF)
        for n in range(0, 1536, 256):
            v["trip1"][w, :, pl.ds(n, 256)] = dot(blocks, v["w1i_v"][:, pl.ds(n, 256)]).astype(BF)
        attend(v["trip1"].at[w], v["mk"].at[w], v["mix"], v["ps1"].at[w])
        projected = dot(v["mix"][...], v["w1o_v"][...]).astype(BF)
        put_pieces(fo, w, rolled_tokens(w) + dot(v["one_t"][...], projected))

    in_one.wait()
    in_w1i.wait()
    in_w1o.wait()
    in_one_t.wait()
    r_a.wait_recv()
    section_one(0)
    f_a = net.send(fo.at[0, pl.ds(1, 1)], lay.at[1, pl.ds(0, 1)], (i, left))
    f_b = net.send(fo.at[0, pl.ds(0, 1)], lay.at[1, pl.ds(3, 1)], (down, left))
    f_c = net.send(fo.at[1, pl.ds(0, 1)], lay.at[0, pl.ds(3, 1)], (down, j))
    if ring:
        gather.forward(0)
    r_b.wait_recv()
    r_c.wait_recv()
    r_d.wait_recv()
    section_one(1)
    f_d = net.send(fo.at[0, pl.ds(2, 2)], lay.at[1, pl.ds(1, 2)], (i, left))

    for copy in in_rest:
        copy.wait()
    cot_a.wait_recv()
    cot_b.wait_recv()
    slabs = []
    for slab in range(24):
        slabs += [v["cot_r"][slab // 12, slab // 3 % 4, slab % 3].astype(F32), jnp.zeros((2, 1024), F32)]
    v["cot2"][0] = dot(v["coa"][...], jnp.concatenate(slabs, axis=0).astype(BF)).astype(BF)
    cot_m = net.send(v["cot2"].at[0], v["cot2"].at[1], (i, mate))

    if ring:
        gather.forward(1)

    def merge_half(h, parts):
        value = dot(v["mer"][...], rows_of(parts).astype(BF))
        for pq in range(4):
            v["mf"][pl.ds(72 * h, 72), pl.ds(512 * pq, 512)] = value[72 * pq : 72 * pq + 72]

    f_c.wait_recv()
    merge_half(0, [fo[1, 1], fo[1, 2], fo[1, 3], lay[0, 3]])
    f_a.wait_recv()
    f_b.wait_recv()
    f_d.wait_recv()
    merge_half(1, [lay[1, g] for g in range(4)])
    if ring:
        gather.swapped(0)
    hat, scale = norm(v["mf"][...])
    v["mn"][...] = hat.astype(BF)
    v["rsm"][...] = jnp.broadcast_to(scale, (144, 128))
    in_wm.wait()
    if ring:
        gather.swapped(1)
        gather.finish()
    for copy in everywhere:
        copy.wait_recv()
    merged = v["mn"][...]
    for n in range(0, 1024, 256):
        v["red"][:, pl.ds(n, 256)] = dot(merged, wmv[:, :, pl.ds(n, 256)].reshape(2048, 256)).astype(BF)
    hat, scale = norm(v["red"][...].astype(F32))
    v["nt"][0] = hat.astype(BF)
    v["rs2"][...] = jnp.broadcast_to(scale, (144, 128))
    n_m = net.send(v["nt"].at[0], v["nt"].at[1], (i, mate))

    own_rows = pl.ds(pl.multiple_of(512 * core, 512), 512)
    far_rows = pl.ds(pl.multiple_of(512 - 512 * core, 512), 512)
    in_w2o.wait()
    cot_m.wait_recv()
    grad_blocks = dot(v["two"][...], v["cot2"][...].reshape(288, 1024)).astype(BF)
    v["dmix2"][...] = dot(grad_blocks, v["w2o_v"][own_rows, :], NT).astype(BF)
    for copy in in_w2i + in_late:
        copy.wait()
    n_m.wait_recv()

    blocks = dot(v["two"][...], v["nt"][...].reshape(288, 1024)).astype(BF)
    for n in range(0, 1536, 256):
        v["trip2"][:, pl.ds(n, 256)] = dot(blocks, v["w2i_v"][:, pl.ds(n, 256)]).astype(BF)
    attend(v["trip2"], v["mk"].at[1], v["mix2"], v["ps2"])
    mixed = dot(v["two_t"][...], v["mix2"][...]).astype(BF)
    v["mxo"][...] = mixed[:144]
    v["mxs"][...] = mixed[144:]
    x_m = net.send(v["mxs"], v["mxr"], (i, mate))

    attend_back(v["trip2"], v["dmix2"], v["ps2"], v["dtrip"])
    back = dot(v["two_t"][...], v["dtrip"][...]).astype(BF)
    for n in range(0, 1024, 256):
        v["pgs"][:, pl.ds(n, 256)] = dot(back[144:], v["w2i_v"][pl.ds(n, 256), :], NT).astype(BF)
    p_m = net.send(v["pgs"], v["pgr"], (i, mate))
    for n in range(0, 1024, 256):
        v["pgo"][:, pl.ds(n, 256)] = dot(back[:144], v["w2i_v"][pl.ds(n, 256), :], NT)
    p_m.wait_recv()
    grad = (v["pgo"][...] + v["pgr"][...].astype(F32)).astype(BF).astype(F32)
    grad = norm_back(grad, v["nt"][0].astype(F32), v["rs2"][:, :1])
    v["gr"][...] = (grad + v["cot2"][0].astype(F32)).astype(BF)
    for b in range(8):
        rows = merge_rows(b)
        v["gmn"][:, pl.ds(256 * b, 256)] = dot(v["gr"][...], rows, NT).astype(BF)
    v["mf"][...] = norm_back(v["gmn"][...].astype(F32), v["mn"][...].astype(F32), v["rsm"][:, :1])

    def unmerge_half(h):
        rows = v["mf"][pl.ds(72 * h, 72), :]
        value = jnp.concatenate([rows[:, 512 * pq : 512 * pq + 512] for pq in range(4)], axis=0).astype(BF)
        value = dot(v["mer_t"][...], value)
        return [value[72 * g : 72 * g + 72].astype(BF) for g in range(4)]

    for g, value in enumerate(unmerge_half(1)):
        gf[1, g] = value
    b_a = net.send(gf.at[1, pl.ds(1, 2)], g1.at[0, pl.ds(2, 2)], (i, right))
    b_b = net.send(gf.at[1, pl.ds(0, 1)], g1.at[0, pl.ds(1, 1)], (i, right))
    b_c = net.send(gf.at[1, pl.ds(3, 1)], g1.at[0, pl.ds(0, 1)], (up, right))
    parts = unmerge_half(0)
    gf[0, 3] = parts[3]
    b_d = net.send(gf.at[0, pl.ds(3, 1)], g1.at[1, pl.ds(0, 1)], (up, j))
    for g in range(3):
        g1[1, g + 1] = parts[g]

    x_m.wait_recv()
    attended = dot(v["mxo"][...], v["w2o_v"][own_rows, :]) + dot(v["mxr"][...], v["w2o_v"][far_rows, :])
    result = (v["red"][...].astype(F32) + attended.astype(BF).astype(F32)).astype(BF)
    slabs = dot(v["coa_t"][...], result)
    for slab in range(24):
        v["s2o"][slab // 12, slab // 3 % 4, slab % 3] = slabs[8 * slab : 8 * slab + 6].astype(BF)
    o_a = net.send(v["s2o"].at[0], out2.at[:, pl.ds(3, 3)], (i, right))
    o_b = net.send(v["s2o"].at[1], out2.at[:, pl.ds(0, 3)], (up, right))

    def section_one_back(w):
        arrived = rows_of([g1[h, 2 * w + g] for h in range(2) for g in range(2)])
        grad_blocks = dot(v["one"][...], arrived.astype(BF)).astype(BF)
        v["dmix"][...] = dot(grad_blocks, v["w1o_v"][...], NT).astype(BF)
        attend_back(v["trip1"].at[w], v["dmix"], v["ps1"].at[w], v["dtrip"])
        grad = dot(v["dtrip"][...], v["w1i_v"][...], NT).astype(BF)
        grad = dot(v["one_t"][...], grad)
        grad = norm_back(grad, v["nrm"][w].astype(F32), v["rs1"][w, :, :1])
        put_pieces(tg, w, grad + rows_of([g1[h, 2 * w + g] for h in range(2) for g in range(2)]))

    b_a.wait_recv()
    section_one_back(1)
    t_a = net.send(tg.at[1, pl.ds(2, 1)], outg.at[0, pl.ds(3, 1)], (i, right))
    t_b = net.send(tg.at[1, pl.ds(3, 1)], outg.at[0, pl.ds(0, 1)], (up, right))
    t_c = net.send(tg.at[0, pl.ds(3, 1)], outg.at[1, pl.ds(0, 1)], (up, j))
    keep_a = net.local(tg.at[0, pl.ds(2, 1)], outg.at[1, pl.ds(3, 1)])
    b_b.wait_recv()
    b_c.wait_recv()
    b_d.wait_recv()
    section_one_back(0)
    t_d = net.send(tg.at[1, pl.ds(0, 2)], outg.at[0, pl.ds(1, 2)], (i, right))
    keep_b = net.local(tg.at[0, pl.ds(0, 2)], outg.at[1, pl.ds(1, 2)])
    for copy in (o_a, o_b, t_a, t_b, t_c, t_d):
        copy.wait_recv()
    keep_a.wait()
    keep_b.wait()
    for copy in net.remotes:
        copy.wait_send()


def local(tokens, cotangent, *weights, lats, lons):
    shapes = dict(SCRATCH, wmv=((lons, 2048 // lons, 1024), BF))
    constants = [jnp.asarray(a) for a in orders()]
    anywhere = pl.BlockSpec(memory_space=pl.ANY)
    out2, outg = pl.pallas_call(
        functools.partial(body, lats, lons),
        out_shape=(jax.ShapeDtypeStruct((4, 6, 6, 1024), BF), jax.ShapeDtypeStruct((2, 4, 72, 512), BF)),
        in_specs=[anywhere] * N_IN,
        out_specs=(anywhere, anywhere),
        scratch_shapes=[pltpu.VMEM(shape, kind) for shape, kind in shapes.values()]
        + [pltpu.SemaphoreType.DMA((24,)), pltpu.SemaphoreType.DMA((N_SEM,)), pltpu.SemaphoreType.DMA((N_SEM,))],
        compiler_params=pltpu.CompilerParams(
            collective_id=0, has_side_effects=True, vmem_limit_bytes=56 * 2**20
        ),
        name="swin",
    )(tokens, cotangent, *weights, *constants)
    grad = outg.reshape(2, 4, 4, 3, 6, 512).transpose(2, 1, 3, 0, 4, 5).reshape(4, 12, 12, 512)
    return out2, grad


def solution(mesh):
    tiles = P(None, "lat", "lon", None)
    return jax.shard_map(
        functools.partial(local, lats=mesh.shape["lat"], lons=mesh.shape["lon"]),
        mesh=mesh,
        in_specs=(tiles, tiles, P(), P(), P("lon", None), P(), P()),
        out_specs=(tiles, tiles),
        check_vma=False,
    )
```

```python
import functools

import jax
import jax.numpy as jnp
import numpy as np
from jax import lax
from jax.experimental import pallas as pl
from jax.experimental.pallas import tpu as pltpu
from jax.sharding import PartitionSpec as P

F32 = jnp.float32
BF = jnp.bfloat16
NT = ((1,), (1,))
TN = ((0,), (0,))
EPS = 1e-05
MESH = pl.DeviceIdType.MESH


def dot(a, b, dims=((1,), (0,))):
    return lax.dot_general(a, b, (dims, ((), ())), preferred_element_type=F32)


def window_place(level, row_half, counters):
    key = ("a", row_half) if level in (1, 2) else (level, row_half)
    start = {("a", 0): 0, ("a", 1): 72, (3, 0): 144, (3, 1): 180, (0, 0): 216, (0, 1): 252}[key]
    taken = counters.get(key, 0)
    counters[key] = taken + 1
    return start + taken


@functools.lru_cache(None)
def orders():
    one = np.zeros((288, 288), np.float32)
    counters = {}
    for row in range(6):
        for col in range(12):
            for lev in range(4):
                one[window_place(lev, row // 3, counters), row * 48 + col * 4 + lev] = 1
    two = np.zeros((288, 288), np.float32)
    counters = {}
    for m in range(2):
        for h in range(2):
            for row in range(6):
                for col in range(3):
                    for lev in range(4):
                        two[window_place(lev, row // 3, counters), m * 144 + h * 72 + row * 12 + col * 4 + lev] = 1
    merge = np.zeros((288, 288), np.float32)
    for p in range(2):
        for q in range(2):
            for row in range(6):
                for col in range(3):
                    for lev in range(4):
                        source = (2 * row + p) * 24 + (2 * col + q) * 4 + lev
                        merge[(p * 2 + q) * 72 + row * 12 + col * 4 + lev, source] = 1
    return tuple(np.asarray(m, dtype=BF) for m in (one, one.T, two, two.T, merge, merge.T))


def head_rows():
    lane = lax.broadcasted_iota(jnp.int32, (1, 256), 1)
    return [jnp.where((lane >= 64 * h) & (lane < 64 * h + 64), 1.0, 0.0).astype(BF) for h in range(4)]


def stack(x, rows):
    pad = jnp.zeros((16, 256), BF)
    parts = []
    for r in rows:
        parts += [x * r, pad]
    return jnp.concatenate(parts, axis=0)


def unstack(y):
    lane = lax.broadcasted_iota(jnp.int32, (144, 256), 1)
    out = y[480:624]
    for h in (2, 1, 0):
        out = jnp.where(lane < 64 * h + 64, y[160 * h : 160 * h + 144], out)
    return out


def attend(trip, mask, mixed, shares):
    rows = head_rows()
    for s in range(2):
        for g in range(2):
            r = pl.ds(144 * s, 144)
            q = trip[r, pl.ds(256 * g, 256)] * jnp.asarray(0.125, BF)
            k = trip[r, pl.ds(512 + 256 * g, 256)]
            v = trip[r, pl.ds(1024 + 256 * g, 256)]
            raised = jnp.exp(dot(k, stack(q, rows), NT) + mask[s])
            p = (raised * (1.0 / jnp.sum(raised, axis=0, keepdims=True))).astype(BF)
            shares[2 * s + g] = p
            mixed[r, pl.ds(256 * g, 256)] = unstack(dot(p, v, TN)).astype(BF)


def attend_back(trip, grad_mixed, shares, grad_trip):
    rows = head_rows()
    for s in range(2):
        for g in range(2):
            r = pl.ds(144 * s, 144)
            q = trip[r, pl.ds(256 * g, 256)] * jnp.asarray(0.125, BF)
            k = trip[r, pl.ds(512 + 256 * g, 256)]
            v = trip[r, pl.ds(1024 + 256 * g, 256)]
            do = stack(grad_mixed[r, pl.ds(256 * g, 256)], rows)
            p = shares[2 * s + g]
            wide = p.astype(F32)
            t = wide * dot(v, do, NT)
            ds = (t - wide * jnp.sum(t, axis=0, keepdims=True)).astype(BF)
            grad_trip[r, pl.ds(1024 + 256 * g, 256)] = dot(p, do).astype(BF)
            grad_trip[r, pl.ds(512 + 256 * g, 256)] = dot(ds, stack(q, rows)).astype(BF)
            grad_trip[r, pl.ds(256 * g, 256)] = (unstack(dot(ds, k, TN)) * 0.125).astype(BF)


def norm(x):
    center = x - jnp.mean(x, axis=-1, keepdims=True)
    scale = lax.rsqrt(jnp.mean(center * center, axis=-1, keepdims=True) + EPS)
    return center * scale, scale


def norm_back(grad, hat, scale):
    first = jnp.mean(grad, axis=-1, keepdims=True)
    second = jnp.mean(grad * hat, axis=-1, keepdims=True)
    return scale * (grad - first - hat * second)


SCRATCH = dict(
    tk=((12, 12, 4, 512), BF),
    nrm=((2, 288, 512), BF),
    rs1=((2, 288, 128), F32),
    trip1=((2, 288, 1536), BF),
    ps1=((2, 4, 144, 640), BF),
    mix=((288, 512), BF),
    mk=((2, 2, 144, 640), F32),
    fo=((12, 12, 4, 512), BF),
    ly=((12, 12, 4, 512), BF),
    mf=((144, 2048), F32),
    mn=((144, 2048), BF),
    rsm=((144, 128), F32),
    red=((144, 1024), BF),
    nt=((2, 144, 1024), BF),
    rs2=((144, 128), F32),
    w1i_v=((512, 1536), BF),
    w1o_v=((512, 512), BF),
    wmv=((16, 128, 1024), BF),
    w2i_v=((1024, 1536), BF),
    w2o_v=((1024, 1024), BF),
    one=((288, 288), BF),
    one_t=((288, 288), BF),
    two=((288, 288), BF),
    two_t=((288, 288), BF),
    mer=((288, 288), BF),
    mer_t=((288, 288), BF),
    cot_r=((6, 6, 4, 1024), BF),
    cot2=((2, 144, 1024), BF),
    trip2=((288, 1536), BF),
    ps2=((4, 144, 640), BF),
    mix2=((288, 512), BF),
    mxo=((144, 512), BF),
    mxs=((144, 512), BF),
    mxr=((144, 512), BF),
    dmix=((288, 512), BF),
    dmix2=((288, 512), BF),
    dtrip=((288, 1536), BF),
    pgs=((144, 1024), BF),
    pgr=((144, 1024), BF),
    pgo=((144, 1024), F32),
    gr=((144, 1024), BF),
    gmn=((144, 2048), BF),
    gf=((12, 12, 4, 512), BF),
    g1=((12, 12, 4, 512), BF),
    tg=((12, 12, 4, 512), BF),
    s2o=((6, 6, 4, 1024), BF),
)
N_IN = 13
N_SEM = 80


class Remote:
    def __init__(self, copy, when):
        self.copy, self.when = copy, when

    def run(self, act, when):
        if when is None:
            act()
        else:
            pl.when(when)(act)

    def start(self):
        self.run(self.copy.start, self.when)

    def wait_send(self):
        self.run(self.copy.wait_send, self.when)

    def wait_recv(self, when=None):
        self.run(self.copy.wait_recv, self.when if when is None else when)


class Copies:
    def __init__(self, local, send, recv):
        self.local_sems, self.send_sems, self.recv_sems = local, send, recv
        self.locals, self.remotes = 0, []

    def local(self, source, target):
        copy = pltpu.make_async_copy(source, target, self.local_sems.at[self.locals])
        self.locals += 1
        copy.start()
        return copy

    def send(self, source, target, device, when=None):
        place = len(self.remotes)
        copy = pltpu.make_async_remote_copy(
            src_ref=source,
            dst_ref=target,
            send_sem=self.send_sems.at[place],
            recv_sem=self.recv_sems.at[place],
            device_id=device,
            device_id_type=MESH,
        )
        remote = Remote(copy, when)
        remote.start()
        self.remotes.append(remote)
        return remote


class Gather:
    def __init__(self, net, wm, wmv, i, j, lats):
        self.net, self.wmv, self.i = net, wmv, i
        x_hi = j // 8
        y2 = j - x_hi * 8
        self.odd = lax.rem(i // 2, 2)
        across = i + 1 - 2 * lax.rem(i, 2)

        def same(k):
            return x_hi * 8 + lax.rem(y2 + 2 * k + 8, 8)

        def other(k):
            return (1 - x_hi) * 8 + lax.rem(y2 + 2 * k + 8, 8)

        def pick(when_odd, when_even):
            return when_odd * self.odd + when_even * (1 - self.odd)

        self.mate = (i, j + 1 - 2 * lax.rem(j, 2))
        self.z_up, self.z_down = (lax.rem(i + 2, lats), j), (lax.rem(i + lats - 2, lats), j)
        self.targets = {
            0: (pick(i, across), pick(same(-1), other(-1))),
            1: (pick(i, across), pick(same(1), other(1))),
            3: (across, other(0)),
        }
        self.onward = (i, same(1))
        self.mine = [pick(same(1), other(1)), pick(same(-1), other(-1)), pick(same(2), other(2)), other(0)]
        self.theirs = [pick(other(1), same(1)), pick(other(-1), same(-1)), pick(other(2), same(2)), other(0)]
        self.partners = [self.z_up, self.z_down, (across, other(0))]
        for step in (-1, 1):
            self.partners += [(i, same(step)), (across, other(step))]
        self.direct, self.from_z, self.to_mate = {}, {}, []
        self.wm, self.j = wm, j

    def part(self, block, row, rows):
        return self.wmv.at[block, pl.ds(row, rows)]

    def when(self, slot, value):
        return None if slot < 3 else self.odd == value

    def start(self):
        for half in range(2):
            rows = pl.ds(64 * half, 64)
            for slot in (1, 3, 0):
                self.direct[slot, half] = self.net.send(
                    self.wm.at[rows], self.wmv.at[self.j, rows], self.targets[slot], when=self.when(slot, 1)
                )
        self.to_mate.append(self.net.send(self.wm, self.wmv.at[self.j], self.mate))

    def forward(self, slot, half):
        self.direct[slot, half].wait_recv()
        block, when = self.mine[slot], self.when(slot, 1)
        whole = self.part(block, 64 * half, 64)
        if slot == 1:
            self.direct[2, half] = self.net.send(whole, whole, self.onward)
        low, high = self.part(block, 64 * half, 32), self.part(block, 64 * half + 32, 32)
        self.from_z[slot, half] = (
            self.net.send(low, low, self.z_up, when=when),
            self.net.send(high, high, self.z_down, when=when),
        )
        if slot < 3:
            self.to_mate.append(self.net.send(whole, whole, self.mate))

    def swapped(self, slot, half):
        for copy in self.from_z[slot, half]:
            copy.wait_recv(self.when(slot, 0))
        whole = self.part(self.theirs[slot], 64 * half, 64)
        self.to_mate.append(self.net.send(whole, whole, self.mate))

    def finish(self):
        for copy in self.to_mate:
            copy.wait_recv()


def body(lats, lons, *refs):
    (tok_in, cot_in, w1i, w1o, wm, w2i, w2o, c1, c1t, c2, c2t, c3, c3t) = refs[:N_IN]
    out2, outg = refs[N_IN : N_IN + 2]
    rest = refs[N_IN + 2 :]
    v = dict(zip(SCRATCH, rest))
    net = Copies(*rest[len(SCRATCH) :])
    tk, fo, ly, g1, gf, tg, wmv = (v[n] for n in ("tk", "fo", "ly", "g1", "gf", "tg", "wmv"))

    i, j = lax.axis_index("lat"), lax.axis_index("lon")
    up, down = lax.rem(i + 1, lats), lax.rem(i + lats - 1, lats)
    right, left = lax.rem(j + 1, lons), lax.rem(j + lons - 1, lons)
    core = lax.rem(j, 2)
    mate = j + 1 - 2 * core
    ring = lons == 16
    partners = [(i, right), (i, left), (up, j), (down, j), (up, right), (down, left)]
    gather = Gather(net, wm, wmv, i, j, lats) if ring else None
    partners += gather.partners if ring else [(i, lax.rem(j + d, lons)) for d in range(1, lons)]

    barrier = pltpu.get_barrier_semaphore()
    for device in partners:
        pl.semaphore_signal(barrier, inc=1, device_id=device, device_id_type=MESH)

    first, later, near, far = pl.ds(0, 3), pl.ds(3, 9), pl.ds(0, 6), pl.ds(6, 6)
    in_tok = net.local(tok_in.at[later, far], tk.at[pl.ds(0, 9), near])
    in_one = net.local(c1, v["one"])
    in_w1i = net.local(w1i, v["w1i_v"])
    in_w1o = net.local(w1o, v["w1o_v"])
    in_one_t = net.local(c1t, v["one_t"])
    in_wm = net.local(wm, wmv.at[j])
    in_rest = [net.local(a, v[n]) for a, n in ((c3, "mer"), (c2, "two"))]
    in_w2i = [
        net.local(
            w2i.at[:, pl.ds(pl.multiple_of(1024 * part + 512 * core, 512), 512)],
            v["w2i_v"].at[:, pl.ds(512 * part, 512)],
        )
        for part in range(3)
    ]
    in_w2o = net.local(w2o, v["w2o_v"])
    in_late = [net.local(a, v[n]) for a, n in ((c2t, "two_t"), (c3t, "mer_t"))]

    pl.semaphore_wait(barrier, len(partners))

    r_a = net.send(tok_in.at[pl.ds(3, 6), near], tk.at[pl.ds(0, 6), far], (i, left))
    r_b = net.send(tok_in.at[pl.ds(9, 3), near], tk.at[pl.ds(6, 3), far], (i, left))
    r_c = net.send(tok_in.at[first, far], tk.at[pl.ds(9, 3), near], (down, j))
    r_d = net.send(tok_in.at[first, near], tk.at[pl.ds(9, 3), far], (down, left))

    depth = wm.shape[0]
    everywhere = []
    if ring:
        gather.start()
    else:
        for d in range(1, lons):
            everywhere.append(net.send(wm, wmv.at[j], (i, lax.rem(j + d, lons))))

    def merge_rows(b):
        if depth <= 256:
            count = 256 // depth
            return wmv[pl.ds(count * b, count)].reshape(256, 1024)
        return wmv[256 * b // depth, pl.ds(256 * b % depth, 256)]

    lane = lax.broadcasted_iota(jnp.int32, (1, 640), 1)
    lane = lane - 160 * (
        (lane >= 160).astype(jnp.int32) + (lane >= 320).astype(jnp.int32) + (lane >= 480).astype(jnp.int32)
    )
    key = lax.broadcasted_iota(jnp.int32, (144, 1), 0)

    def quarter(index):
        return (index >= 36).astype(jnp.int32) + (index >= 72).astype(jnp.int32) + (index >= 108).astype(jnp.int32)

    pad = lane >= 144
    half_mask = jnp.where(((key >= 72) == (lane >= 72)) | pad, 0.0, -1e30)
    quarter_mask = jnp.where((quarter(key) == quarter(lane)) | pad, 0.0, -1e30)
    last = jnp.broadcast_to(i, (144, 640)) == lats - 1
    v["mk"][0, 0] = jnp.zeros((144, 640), F32)
    v["mk"][0, 1] = half_mask
    v["mk"][1, 0] = jnp.where(last, half_mask, 0.0)
    v["mk"][1, 1] = jnp.where(last, quarter_mask, half_mask)

    def window_rows(ref, w):
        return ref[pl.ds(6 * w, 6)].astype(F32).reshape(288, 512)

    def section_one(w, between):
        hat, scale = norm(window_rows(tk, w))
        normed = hat.astype(BF)
        v["nrm"][w] = normed
        v["rs1"][w] = jnp.broadcast_to(scale, (288, 128))
        blocks = dot(v["one"][...], normed).astype(BF)
        for n in range(0, 1536, 256):
            v["trip1"][w, :, pl.ds(n, 256)] = dot(blocks, v["w1i_v"][:, pl.ds(n, 256)]).astype(BF)
        pump(between)
        attend(v["trip1"].at[w], v["mk"].at[w], v["mix"], v["ps1"].at[w])
        projected = dot(v["mix"][...], v["w1o_v"][...]).astype(BF)
        value = window_rows(tk, w) + dot(v["one_t"][...], projected)
        fo[pl.ds(6 * w, 6)] = value.reshape(6, 12, 4, 512).astype(BF)

    def pump(steps):
        if ring:
            for act, slot, half in steps:
                getattr(gather, act)(slot, half)

    in_one.wait()
    in_w1i.wait()
    in_w1o.wait()
    in_one_t.wait()
    in_tok.wait()
    r_a.wait_recv()
    pump([("forward", 1, 0)])
    section_one(0, [("forward", 3, 0)])
    f_a = net.send(fo.at[pl.ds(3, 3), near], ly.at[pl.ds(0, 3), far], (i, left))
    f_b = net.send(fo.at[first, near], ly.at[pl.ds(9, 3), far], (down, left))
    f_c = net.send(fo.at[first, far], ly.at[pl.ds(9, 3), near], (down, j))
    pump([("forward", 0, 0), ("forward", 1, 1)])
    r_b.wait_recv()
    r_c.wait_recv()
    r_d.wait_recv()
    section_one(1, [("forward", 2, 0), ("forward", 3, 1)])
    f_d = net.send(fo.at[pl.ds(6, 6), near], ly.at[pl.ds(3, 6), far], (i, left))
    ly[pl.ds(0, 9), near] = fo[later, far]
    pump([("forward", 0, 1), ("swapped", 1, 0), ("swapped", 3, 0), ("swapped", 0, 0), ("forward", 2, 1)])
    cot_a = net.send(cot_in.at[pl.ds(3, 3)], v["cot_r"].at[pl.ds(0, 3)], (i, left))
    cot_b = net.send(cot_in.at[pl.ds(0, 3)], v["cot_r"].at[pl.ds(3, 3)], (down, left))
    for copy in in_rest:
        copy.wait()

    def merge_half(h):
        value = dot(v["mer"][...], ly[:, pl.ds(6 * h, 6)].astype(F32).reshape(288, 512).astype(BF))
        for pq in range(4):
            v["mf"][pl.ds(72 * h, 72), pl.ds(512 * pq, 512)] = value[72 * pq : 72 * pq + 72]

    f_c.wait_recv()
    merge_half(0)
    f_a.wait_recv()
    f_b.wait_recv()
    f_d.wait_recv()
    merge_half(1)
    pump([("swapped", 2, 0), ("swapped", 1, 1), ("swapped", 3, 1), ("swapped", 0, 1)])
    hat, scale = norm(v["mf"][...])
    v["mn"][...] = hat.astype(BF)
    v["rsm"][...] = jnp.broadcast_to(scale, (144, 128))
    pump([("swapped", 2, 1)])

    cot_a.wait_recv()
    cot_b.wait_recv()
    halves = [v["cot_r"][:, pl.ds(3 * h, 3)].astype(F32).reshape(72, 1024) for h in range(2)]
    v["cot2"][0] = jnp.concatenate(halves, axis=0).astype(BF)
    cot_m = net.send(v["cot2"].at[0], v["cot2"].at[1], (i, mate))

    in_wm.wait()
    if ring:
        gather.finish()
    for copy in everywhere:
        copy.wait_recv()
    merged = v["mn"][...]
    for n in range(0, 1024, 256):
        v["red"][:, pl.ds(n, 256)] = dot(merged, wmv[:, :, pl.ds(n, 256)].reshape(2048, 256)).astype(BF)
    hat, scale = norm(v["red"][...].astype(F32))
    v["nt"][0] = hat.astype(BF)
    v["rs2"][...] = jnp.broadcast_to(scale, (144, 128))
    n_m = net.send(v["nt"].at[0], v["nt"].at[1], (i, mate))

    own_rows = pl.ds(pl.multiple_of(512 * core, 512), 512)
    far_rows = pl.ds(pl.multiple_of(512 - 512 * core, 512), 512)
    in_w2o.wait()
    cot_m.wait_recv()
    grad_blocks = dot(v["two"][...], v["cot2"][...].reshape(288, 1024)).astype(BF)
    v["dmix2"][...] = dot(grad_blocks, v["w2o_v"][own_rows, :], NT).astype(BF)
    for copy in in_w2i + in_late:
        copy.wait()
    n_m.wait_recv()

    blocks = dot(v["two"][...], v["nt"][...].reshape(288, 1024)).astype(BF)
    for n in range(0, 1536, 256):
        v["trip2"][:, pl.ds(n, 256)] = dot(blocks, v["w2i_v"][:, pl.ds(n, 256)]).astype(BF)
    attend(v["trip2"], v["mk"].at[1], v["mix2"], v["ps2"])
    mixed = dot(v["two_t"][...], v["mix2"][...]).astype(BF)
    v["mxo"][...] = mixed[:144]
    v["mxs"][...] = mixed[144:]
    x_m = net.send(v["mxs"], v["mxr"], (i, mate))

    attend_back(v["trip2"], v["dmix2"], v["ps2"], v["dtrip"])
    back = dot(v["two_t"][...], v["dtrip"][...]).astype(BF)
    for n in range(0, 1024, 256):
        v["pgs"][:, pl.ds(n, 256)] = dot(back[144:], v["w2i_v"][pl.ds(n, 256), :], NT).astype(BF)
    p_m = net.send(v["pgs"], v["pgr"], (i, mate))
    for n in range(0, 1024, 256):
        v["pgo"][:, pl.ds(n, 256)] = dot(back[:144], v["w2i_v"][pl.ds(n, 256), :], NT)
    p_m.wait_recv()
    grad = (v["pgo"][...] + v["pgr"][...].astype(F32)).astype(BF).astype(F32)
    grad = norm_back(grad, v["nt"][0].astype(F32), v["rs2"][:, :1])
    v["gr"][...] = (grad + v["cot2"][0].astype(F32)).astype(BF)
    for b in range(8):
        rows = merge_rows(b)
        v["gmn"][:, pl.ds(256 * b, 256)] = dot(v["gr"][...], rows, NT).astype(BF)
    v["mf"][...] = norm_back(v["gmn"][...].astype(F32), v["mn"][...].astype(F32), v["rsm"][:, :1])

    def unmerge_half(h):
        rows = v["mf"][pl.ds(72 * h, 72), :]
        value = jnp.concatenate([rows[:, 512 * pq : 512 * pq + 512] for pq in range(4)], axis=0).astype(BF)
        return dot(v["mer_t"][...], value).reshape(12, 6, 4, 512).astype(BF)

    gf[:, far] = unmerge_half(1)
    b_a = net.send(gf.at[pl.ds(3, 6), far], g1.at[pl.ds(6, 6), near], (i, right))
    b_b = net.send(gf.at[first, far], g1.at[pl.ds(3, 3), near], (i, right))
    b_c = net.send(gf.at[pl.ds(9, 3), far], g1.at[first, near], (up, right))
    value = unmerge_half(0)
    gf[pl.ds(9, 3), near] = value[9:]
    b_d = net.send(gf.at[pl.ds(9, 3), near], g1.at[first, far], (up, j))
    g1[later, far] = value[:9]

    x_m.wait_recv()
    attended = dot(v["mxo"][...], v["w2o_v"][own_rows, :]) + dot(v["mxr"][...], v["w2o_v"][far_rows, :])
    result = v["red"][...].astype(F32) + attended.astype(BF).astype(F32)
    for h in range(2):
        v["s2o"][:, pl.ds(3 * h, 3)] = result[72 * h : 72 * h + 72].reshape(6, 3, 4, 1024).astype(BF)
    o_a = net.send(v["s2o"].at[pl.ds(0, 3)], out2.at[pl.ds(3, 3)], (i, right))
    o_b = net.send(v["s2o"].at[pl.ds(3, 3)], out2.at[pl.ds(0, 3)], (up, right))

    def section_one_back(w):
        grad_blocks = dot(v["one"][...], window_rows(g1, w).astype(BF)).astype(BF)
        v["dmix"][...] = dot(grad_blocks, v["w1o_v"][...], NT).astype(BF)
        attend_back(v["trip1"].at[w], v["dmix"], v["ps1"].at[w], v["dtrip"])
        grad = dot(v["dtrip"][...], v["w1i_v"][...], NT).astype(BF)
        grad = dot(v["one_t"][...], grad)
        grad = norm_back(grad, v["nrm"][w].astype(F32), v["rs1"][w, :, :1])
        tg[pl.ds(6 * w, 6)] = (grad + window_rows(g1, w)).reshape(6, 12, 4, 512).astype(BF)

    b_a.wait_recv()
    section_one_back(1)
    t_a = net.send(tg.at[pl.ds(6, 3), far], outg.at[pl.ds(9, 3), near], (i, right))
    t_b = net.send(tg.at[pl.ds(9, 3), far], outg.at[first, near], (up, right))
    t_c = net.send(tg.at[pl.ds(9, 3), near], outg.at[first, far], (up, j))
    keep_a = net.local(tg.at[pl.ds(6, 3), near], outg.at[pl.ds(9, 3), far])
    b_b.wait_recv()
    b_c.wait_recv()
    b_d.wait_recv()
    section_one_back(0)
    t_d = net.send(tg.at[pl.ds(0, 6), far], outg.at[pl.ds(3, 6), near], (i, right))
    keep_b = net.local(tg.at[pl.ds(0, 6), near], outg.at[pl.ds(3, 6), far])
    for copy in (o_a, o_b, t_a, t_b, t_c, t_d):
        copy.wait_recv()
    keep_a.wait()
    keep_b.wait()
    for copy in net.remotes:
        copy.wait_send()


def local(tokens, cotangent, *weights, lats, lons):
    shapes = dict(SCRATCH, wmv=((lons, 2048 // lons, 1024), BF))
    constants = [jnp.asarray(a) for a in orders()]
    anywhere = pl.BlockSpec(memory_space=pl.ANY)
    out2, outg = pl.pallas_call(
        functools.partial(body, lats, lons),
        out_shape=(jax.ShapeDtypeStruct((6, 6, 4, 1024), BF), jax.ShapeDtypeStruct((12, 12, 4, 512), BF)),
        in_specs=[anywhere] * N_IN,
        out_specs=(anywhere, anywhere),
        scratch_shapes=[pltpu.VMEM(shape, kind) for shape, kind in shapes.values()]
        + [pltpu.SemaphoreType.DMA((24,)), pltpu.SemaphoreType.DMA((N_SEM,)), pltpu.SemaphoreType.DMA((N_SEM,))],
        compiler_params=pltpu.CompilerParams(
            collective_id=0, has_side_effects=True, vmem_limit_bytes=56 * 2**20
        ),
        name="swin",
    )(tokens.transpose(1, 2, 0, 3), cotangent.transpose(1, 2, 0, 3), *weights, *constants)
    return out2.transpose(2, 0, 1, 3), outg.transpose(2, 0, 1, 3)


def solution(mesh):
    tiles = P(None, "lat", "lon", None)
    return jax.shard_map(
        functools.partial(local, lats=mesh.shape["lat"], lons=mesh.shape["lon"]),
        mesh=mesh,
        in_specs=(tiles, tiles, P(), P(), P("lon", None), P(), P()),
        out_specs=(tiles, tiles),
        check_vma=False,
    )
```

```python
import functools

import jax
import jax.numpy as jnp
import numpy as np
from jax import lax
from jax.experimental import pallas as pl
from jax.experimental.pallas import tpu as pltpu
from jax.sharding import PartitionSpec as P

F32 = jnp.float32
BF = jnp.bfloat16
NT = ((1,), (1,))
TN = ((0,), (0,))
EPS = 1e-05
MESH = pl.DeviceIdType.MESH


def dot(a, b, dims=((1,), (0,))):
    return lax.dot_general(a, b, (dims, ((), ())), preferred_element_type=F32)


def window_place(level, row_half, counters):
    key = ("a", row_half) if level in (1, 2) else (level, row_half)
    start = {("a", 0): 0, ("a", 1): 72, (3, 0): 144, (3, 1): 180, (0, 0): 216, (0, 1): 252}[key]
    taken = counters.get(key, 0)
    counters[key] = taken + 1
    return start + taken


@functools.lru_cache(None)
def orders():
    one = np.zeros((288, 288), np.float32)
    counters = {}
    for row in range(6):
        for col in range(12):
            for lev in range(4):
                one[window_place(lev, row // 3, counters), row * 48 + col * 4 + lev] = 1
    two = np.zeros((288, 288), np.float32)
    counters = {}
    for m in range(2):
        for h in range(2):
            for row in range(6):
                for col in range(3):
                    for lev in range(4):
                        two[window_place(lev, row // 3, counters), m * 144 + h * 72 + row * 12 + col * 4 + lev] = 1
    merge = np.zeros((288, 288), np.float32)
    for p in range(2):
        for q in range(2):
            for row in range(6):
                for col in range(3):
                    for lev in range(4):
                        source = (2 * row + p) * 24 + (2 * col + q) * 4 + lev
                        merge[(p * 2 + q) * 72 + row * 12 + col * 4 + lev, source] = 1
    return tuple(np.asarray(m, dtype=BF) for m in (one, one.T, two, two.T, merge, merge.T))


def head_rows():
    lane = lax.broadcasted_iota(jnp.int32, (1, 256), 1)
    return [jnp.where((lane >= 64 * h) & (lane < 64 * h + 64), 1.0, 0.0).astype(BF) for h in range(4)]


def stack(x, rows):
    pad = jnp.zeros((16, 256), BF)
    parts = []
    for r in rows:
        parts += [x * r, pad]
    return jnp.concatenate(parts, axis=0)


def unstack(y):
    lane = lax.broadcasted_iota(jnp.int32, (144, 256), 1)
    out = y[480:624]
    for h in (2, 1, 0):
        out = jnp.where(lane < 64 * h + 64, y[160 * h : 160 * h + 144], out)
    return out


def attend(trip, mask, mixed, shares):
    rows = head_rows()
    for s in range(2):
        for g in range(2):
            r = pl.ds(144 * s, 144)
            q = trip[r, pl.ds(256 * g, 256)] * jnp.asarray(0.125, BF)
            k = trip[r, pl.ds(512 + 256 * g, 256)]
            v = trip[r, pl.ds(1024 + 256 * g, 256)]
            raised = jnp.exp(dot(k, stack(q, rows), NT) + mask[s])
            p = (raised * (1.0 / jnp.sum(raised, axis=0, keepdims=True))).astype(BF)
            shares[2 * s + g] = p
            mixed[r, pl.ds(256 * g, 256)] = unstack(dot(p, v, TN)).astype(BF)


def attend_back(trip, grad_mixed, shares, grad_trip):
    rows = head_rows()
    for s in range(2):
        for g in range(2):
            r = pl.ds(144 * s, 144)
            q = trip[r, pl.ds(256 * g, 256)] * jnp.asarray(0.125, BF)
            k = trip[r, pl.ds(512 + 256 * g, 256)]
            v = trip[r, pl.ds(1024 + 256 * g, 256)]
            do = stack(grad_mixed[r, pl.ds(256 * g, 256)], rows)
            p = shares[2 * s + g]
            wide = p.astype(F32)
            t = wide * dot(v, do, NT)
            ds = (t - wide * jnp.sum(t, axis=0, keepdims=True)).astype(BF)
            grad_trip[r, pl.ds(1024 + 256 * g, 256)] = dot(p, do).astype(BF)
            grad_trip[r, pl.ds(512 + 256 * g, 256)] = dot(ds, stack(q, rows)).astype(BF)
            grad_trip[r, pl.ds(256 * g, 256)] = (unstack(dot(ds, k, TN)) * 0.125).astype(BF)


def norm(x):
    center = x - jnp.mean(x, axis=-1, keepdims=True)
    scale = lax.rsqrt(jnp.mean(center * center, axis=-1, keepdims=True) + EPS)
    return center * scale, scale


def norm_back(grad, hat, scale):
    first = jnp.mean(grad, axis=-1, keepdims=True)
    second = jnp.mean(grad * hat, axis=-1, keepdims=True)
    return scale * (grad - first - hat * second)


SCRATCH = dict(
    tk=((12, 12, 4, 512), BF),
    nrm=((2, 288, 512), BF),
    rs1=((2, 288, 128), F32),
    trip1=((2, 288, 1536), BF),
    ps1=((2, 4, 144, 640), BF),
    mix=((288, 512), BF),
    mk=((2, 2, 144, 640), F32),
    fo=((12, 12, 4, 512), BF),
    ly=((12, 12, 4, 512), BF),
    mf=((144, 2048), F32),
    mn=((144, 2048), BF),
    rsm=((144, 128), F32),
    red=((144, 1024), BF),
    nt=((2, 144, 1024), BF),
    rs2=((144, 128), F32),
    w1i_v=((512, 1536), BF),
    w1o_v=((512, 512), BF),
    wmv=((16, 128, 1024), BF),
    w2i_v=((1024, 1536), BF),
    w2o_v=((1024, 1024), BF),
    one=((288, 288), BF),
    one_t=((288, 288), BF),
    two=((288, 288), BF),
    two_t=((288, 288), BF),
    mer=((288, 288), BF),
    mer_t=((288, 288), BF),
    cot_r=((6, 6, 4, 1024), BF),
    cot2=((2, 144, 1024), BF),
    trip2=((288, 1536), BF),
    ps2=((4, 144, 640), BF),
    mix2=((288, 512), BF),
    mxo=((144, 512), BF),
    mxs=((144, 512), BF),
    mxr=((144, 512), BF),
    dmix=((288, 512), BF),
    dmix2=((288, 512), BF),
    dtrip=((288, 1536), BF),
    pgs=((144, 1024), BF),
    pgr=((144, 1024), BF),
    pgo=((144, 1024), F32),
    gr=((144, 1024), BF),
    gmn=((144, 2048), BF),
    gf=((12, 12, 4, 512), BF),
    g1=((12, 12, 4, 512), BF),
    tg=((12, 12, 4, 512), BF),
    s2o=((6, 6, 4, 1024), BF),
)
N_IN = 13
N_SEM = 80


class Remote:
    def __init__(self, copy, when):
        self.copy, self.when = copy, when

    def run(self, act, when):
        if when is None:
            act()
        else:
            pl.when(when)(act)

    def start(self):
        self.run(self.copy.start, self.when)

    def wait_send(self):
        self.run(self.copy.wait_send, self.when)

    def wait_recv(self, when=None):
        self.run(self.copy.wait_recv, self.when if when is None else when)


class Copies:
    def __init__(self, local, send, recv):
        self.local_sems, self.send_sems, self.recv_sems = local, send, recv
        self.locals, self.remotes = 0, []

    def local(self, source, target):
        copy = pltpu.make_async_copy(source, target, self.local_sems.at[self.locals])
        self.locals += 1
        copy.start()
        return copy

    def send(self, source, target, device, when=None):
        place = len(self.remotes)
        copy = pltpu.make_async_remote_copy(
            src_ref=source,
            dst_ref=target,
            send_sem=self.send_sems.at[place],
            recv_sem=self.recv_sems.at[place],
            device_id=device,
            device_id_type=MESH,
        )
        remote = Remote(copy, when)
        remote.start()
        self.remotes.append(remote)
        return remote


class Gather:
    def __init__(self, net, wm, wmv, i, j, lats):
        self.net, self.wmv, self.i = net, wmv, i
        x_hi = j // 8
        y2 = j - x_hi * 8
        self.odd = lax.rem(i // 2, 2)
        across = i + 1 - 2 * lax.rem(i, 2)

        def same(k):
            return x_hi * 8 + lax.rem(y2 + 2 * k + 8, 8)

        def other(k):
            return (1 - x_hi) * 8 + lax.rem(y2 + 2 * k + 8, 8)

        def pick(when_odd, when_even):
            return when_odd * self.odd + when_even * (1 - self.odd)

        self.mate = (i, j + 1 - 2 * lax.rem(j, 2))
        self.z_up, self.z_down = (lax.rem(i + 2, lats), j), (lax.rem(i + lats - 2, lats), j)
        self.targets = {
            0: (pick(i, across), pick(same(-1), other(-1))),
            1: (pick(i, across), pick(same(1), other(1))),
            3: (across, other(0)),
        }
        self.onward = (i, same(1))
        self.mine = [pick(same(1), other(1)), pick(same(-1), other(-1)), pick(same(2), other(2)), other(0)]
        self.theirs = [pick(other(1), same(1)), pick(other(-1), same(-1)), pick(other(2), same(2)), other(0)]
        self.partners = [self.z_up, self.z_down, (across, other(0))]
        for step in (-1, 1):
            self.partners += [(i, same(step)), (across, other(step))]
        self.direct, self.from_z, self.to_mate = {}, {}, []
        self.wm, self.j = wm, j

    def part(self, block, row, rows):
        return self.wmv.at[block, pl.ds(row, rows)]

    def when(self, slot, value):
        return None if slot < 3 else self.odd == value

    def start(self):
        for half in range(2):
            rows = pl.ds(64 * half, 64)
            for slot in (1, 3, 0):
                self.direct[slot, half] = self.net.send(
                    self.wm.at[rows], self.wmv.at[self.j, rows], self.targets[slot], when=self.when(slot, 1)
                )
        self.to_mate.append(self.net.send(self.wm, self.wmv.at[self.j], self.mate))

    def forward(self, slot, half):
        self.direct[slot, half].wait_recv()
        block, when = self.mine[slot], self.when(slot, 1)
        whole = self.part(block, 64 * half, 64)
        if slot == 1:
            self.direct[2, half] = self.net.send(whole, whole, self.onward)
        low, high = self.part(block, 64 * half, 32), self.part(block, 64 * half + 32, 32)
        self.from_z[slot, half] = (
            self.net.send(low, low, self.z_up, when=when),
            self.net.send(high, high, self.z_down, when=when),
        )
        if slot < 3:
            self.to_mate.append(self.net.send(whole, whole, self.mate))

    def swapped(self, slot, half):
        for copy in self.from_z[slot, half]:
            copy.wait_recv(self.when(slot, 0))
        whole = self.part(self.theirs[slot], 64 * half, 64)
        self.to_mate.append(self.net.send(whole, whole, self.mate))

    def finish(self):
        for copy in self.to_mate:
            copy.wait_recv()


def body(lats, lons, *refs):
    (tok_in, cot_in, w1i, w1o, wm, w2i, w2o, c1, c1t, c2, c2t, c3, c3t) = refs[:N_IN]
    out2, outg = refs[N_IN : N_IN + 2]
    rest = refs[N_IN + 2 :]
    v = dict(zip(SCRATCH, rest))
    net = Copies(*rest[len(SCRATCH) :])
    tk, fo, ly, g1, gf, tg, wmv = (v[n] for n in ("tk", "fo", "ly", "g1", "gf", "tg", "wmv"))

    i, j = lax.axis_index("lat"), lax.axis_index("lon")
    up, down = lax.rem(i + 1, lats), lax.rem(i + lats - 1, lats)
    right, left = lax.rem(j + 1, lons), lax.rem(j + lons - 1, lons)
    core = lax.rem(j, 2)
    mate = j + 1 - 2 * core
    ring = lons == 16
    partners = [(i, right), (i, left), (up, j), (down, j), (up, right), (down, left)]
    gather = Gather(net, wm, wmv, i, j, lats) if ring else None
    partners += gather.partners if ring else [(i, lax.rem(j + d, lons)) for d in range(1, lons)]

    barrier = pltpu.get_barrier_semaphore()
    for device in partners:
        pl.semaphore_signal(barrier, inc=1, device_id=device, device_id_type=MESH)

    first, later, near, far = pl.ds(0, 3), pl.ds(3, 9), pl.ds(0, 6), pl.ds(6, 6)
    in_tok = net.local(tok_in.at[later, far], tk.at[pl.ds(0, 9), near])
    in_one = net.local(c1, v["one"])
    in_w1i = net.local(w1i, v["w1i_v"])
    in_w1o = net.local(w1o, v["w1o_v"])
    in_one_t = net.local(c1t, v["one_t"])
    in_wm = net.local(wm, wmv.at[j])
    in_rest = [net.local(a, v[n]) for a, n in ((c3, "mer"), (c2, "two"))]
    in_w2i = [
        net.local(
            w2i.at[:, pl.ds(pl.multiple_of(1024 * part + 512 * core, 512), 512)],
            v["w2i_v"].at[:, pl.ds(512 * part, 512)],
        )
        for part in range(3)
    ]
    in_w2o = net.local(w2o, v["w2o_v"])
    in_late = [net.local(a, v[n]) for a, n in ((c2t, "two_t"), (c3t, "mer_t"))]

    pl.semaphore_wait(barrier, len(partners))

    r_a = net.send(tok_in.at[pl.ds(3, 6), near], tk.at[pl.ds(0, 6), far], (i, left))
    r_b = net.send(tok_in.at[pl.ds(9, 3), near], tk.at[pl.ds(6, 3), far], (i, left))
    r_c = net.send(tok_in.at[first, far], tk.at[pl.ds(9, 3), near], (down, j))
    r_d = net.send(tok_in.at[first, near], tk.at[pl.ds(9, 3), far], (down, left))

    depth = wm.shape[0]
    everywhere = []
    if ring:
        gather.start()
    else:
        for d in range(1, lons):
            everywhere.append(net.send(wm, wmv.at[j], (i, lax.rem(j + d, lons))))

    def merge_rows(b):
        if depth <= 256:
            count = 256 // depth
            return wmv[pl.ds(count * b, count)].reshape(256, 1024)
        return wmv[256 * b // depth, pl.ds(256 * b % depth, 256)]

    lane = lax.broadcasted_iota(jnp.int32, (1, 640), 1)
    lane = lane - 160 * (
        (lane >= 160).astype(jnp.int32) + (lane >= 320).astype(jnp.int32) + (lane >= 480).astype(jnp.int32)
    )
    key = lax.broadcasted_iota(jnp.int32, (144, 1), 0)

    def quarter(index):
        return (index >= 36).astype(jnp.int32) + (index >= 72).astype(jnp.int32) + (index >= 108).astype(jnp.int32)

    pad = lane >= 144
    half_mask = jnp.where(((key >= 72) == (lane >= 72)) | pad, 0.0, -1e30)
    quarter_mask = jnp.where((quarter(key) == quarter(lane)) | pad, 0.0, -1e30)
    last = jnp.broadcast_to(i, (144, 640)) == lats - 1
    v["mk"][0, 0] = jnp.zeros((144, 640), F32)
    v["mk"][0, 1] = half_mask
    v["mk"][1, 0] = jnp.where(last, half_mask, 0.0)
    v["mk"][1, 1] = jnp.where(last, quarter_mask, half_mask)

    def window_rows(ref, w):
        return ref[pl.ds(6 * w, 6)].astype(F32).reshape(288, 512)

    def section_one(w, between):
        hat, scale = norm(window_rows(tk, w))
        normed = hat.astype(BF)
        v["nrm"][w] = normed
        v["rs1"][w] = jnp.broadcast_to(scale, (288, 128))
        blocks = dot(v["one"][...], normed).astype(BF)
        for n in range(0, 1536, 256):
            v["trip1"][w, :, pl.ds(n, 256)] = dot(blocks, v["w1i_v"][:, pl.ds(n, 256)]).astype(BF)
        pump(between)
        attend(v["trip1"].at[w], v["mk"].at[w], v["mix"], v["ps1"].at[w])
        projected = dot(v["mix"][...], v["w1o_v"][...]).astype(BF)
        value = window_rows(tk, w) + dot(v["one_t"][...], projected)
        fo[pl.ds(6 * w, 6)] = value.reshape(6, 12, 4, 512).astype(BF)

    def pump(steps):
        if ring:
            for act, slot, half in steps:
                getattr(gather, act)(slot, half)

    in_one.wait()
    in_w1i.wait()
    in_w1o.wait()
    in_one_t.wait()
    in_tok.wait()
    r_a.wait_recv()
    pump([("forward", 1, 0)])
    section_one(0, [("forward", 3, 0)])
    f_a = net.send(fo.at[pl.ds(3, 3), near], ly.at[pl.ds(0, 3), far], (i, left))
    f_b = net.send(fo.at[first, near], ly.at[pl.ds(9, 3), far], (down, left))
    f_c = net.send(fo.at[first, far], ly.at[pl.ds(9, 3), near], (down, j))
    pump([("forward", 0, 0), ("forward", 1, 1)])
    r_b.wait_recv()
    r_c.wait_recv()
    r_d.wait_recv()
    section_one(1, [("forward", 2, 0), ("forward", 3, 1)])
    f_d = net.send(fo.at[pl.ds(6, 6), near], ly.at[pl.ds(3, 6), far], (i, left))
    ly[pl.ds(0, 9), near] = fo[later, far]
    pump([("forward", 0, 1), ("swapped", 1, 0), ("swapped", 3, 0), ("swapped", 0, 0), ("forward", 2, 1)])
    cot_a = net.send(cot_in.at[pl.ds(3, 3)], v["cot_r"].at[pl.ds(0, 3)], (i, left))
    cot_b = net.send(cot_in.at[pl.ds(0, 3)], v["cot_r"].at[pl.ds(3, 3)], (down, left))
    for copy in in_rest:
        copy.wait()

    def merge_half(h):
        value = dot(v["mer"][...], ly[:, pl.ds(6 * h, 6)].astype(F32).reshape(288, 512).astype(BF))
        for pq in range(4):
            v["mf"][pl.ds(72 * h, 72), pl.ds(512 * pq, 512)] = value[72 * pq : 72 * pq + 72]

    f_c.wait_recv()
    merge_half(0)
    f_a.wait_recv()
    f_b.wait_recv()
    f_d.wait_recv()
    merge_half(1)
    pump([("swapped", 2, 0), ("swapped", 1, 1), ("swapped", 3, 1), ("swapped", 0, 1)])
    hat, scale = norm(v["mf"][...])
    v["mn"][...] = hat.astype(BF)
    v["rsm"][...] = jnp.broadcast_to(scale, (144, 128))
    pump([("swapped", 2, 1)])

    cot_a.wait_recv()
    cot_b.wait_recv()
    halves = [v["cot_r"][:, pl.ds(3 * h, 3)].astype(F32).reshape(72, 1024) for h in range(2)]
    v["cot2"][0] = jnp.concatenate(halves, axis=0).astype(BF)
    cot_m = net.send(v["cot2"].at[0], v["cot2"].at[1], (i, mate))

    in_wm.wait()
    if ring:
        gather.finish()
    for copy in everywhere:
        copy.wait_recv()
    merged = v["mn"][...]
    for n in range(0, 1024, 256):
        v["red"][:, pl.ds(n, 256)] = dot(merged, wmv[:, :, pl.ds(n, 256)].reshape(2048, 256)).astype(BF)
    hat, scale = norm(v["red"][...].astype(F32))
    v["nt"][0] = hat.astype(BF)
    v["rs2"][...] = jnp.broadcast_to(scale, (144, 128))
    n_m = net.send(v["nt"].at[0], v["nt"].at[1], (i, mate))

    own_rows = pl.ds(pl.multiple_of(512 * core, 512), 512)
    far_rows = pl.ds(pl.multiple_of(512 - 512 * core, 512), 512)
    in_w2o.wait()
    cot_m.wait_recv()
    grad_blocks = dot(v["two"][...], v["cot2"][...].reshape(288, 1024)).astype(BF)
    v["dmix2"][...] = dot(grad_blocks, v["w2o_v"][own_rows, :], NT).astype(BF)
    for copy in in_w2i + in_late:
        copy.wait()
    n_m.wait_recv()

    blocks = dot(v["two"][...], v["nt"][...].reshape(288, 1024)).astype(BF)
    for n in range(0, 1536, 256):
        v["trip2"][:, pl.ds(n, 256)] = dot(blocks, v["w2i_v"][:, pl.ds(n, 256)]).astype(BF)
    attend(v["trip2"], v["mk"].at[1], v["mix2"], v["ps2"])
    mixed = dot(v["two_t"][...], v["mix2"][...]).astype(BF)
    v["mxo"][...] = mixed[:144]
    v["mxs"][...] = mixed[144:]
    x_m = net.send(v["mxs"], v["mxr"], (i, mate))

    attend_back(v["trip2"], v["dmix2"], v["ps2"], v["dtrip"])
    back = dot(v["two_t"][...], v["dtrip"][...]).astype(BF)
    for n in range(0, 1024, 256):
        v["pgs"][:, pl.ds(n, 256)] = dot(back[144:], v["w2i_v"][pl.ds(n, 256), :], NT).astype(BF)
    p_m = net.send(v["pgs"], v["pgr"], (i, mate))
    for n in range(0, 1024, 256):
        v["pgo"][:, pl.ds(n, 256)] = dot(back[:144], v["w2i_v"][pl.ds(n, 256), :], NT)
    p_m.wait_recv()
    grad = (v["pgo"][...] + v["pgr"][...].astype(F32)).astype(BF).astype(F32)
    grad = norm_back(grad, v["nt"][0].astype(F32), v["rs2"][:, :1])
    v["gr"][...] = (grad + v["cot2"][0].astype(F32)).astype(BF)
    for b in range(8):
        rows = merge_rows(b)
        v["gmn"][:, pl.ds(256 * b, 256)] = dot(v["gr"][...], rows, NT).astype(BF)
    v["mf"][...] = norm_back(v["gmn"][...].astype(F32), v["mn"][...].astype(F32), v["rsm"][:, :1])

    def unmerge_half(h):
        rows = v["mf"][pl.ds(72 * h, 72), :]
        value = jnp.concatenate([rows[:, 512 * pq : 512 * pq + 512] for pq in range(4)], axis=0).astype(BF)
        return dot(v["mer_t"][...], value).reshape(12, 6, 4, 512).astype(BF)

    gf[:, far] = unmerge_half(1)
    b_a = net.send(gf.at[pl.ds(3, 6), far], g1.at[pl.ds(6, 6), near], (i, right))
    b_b = net.send(gf.at[first, far], g1.at[pl.ds(3, 3), near], (i, right))
    b_c = net.send(gf.at[pl.ds(9, 3), far], g1.at[first, near], (up, right))
    value = unmerge_half(0)
    gf[pl.ds(9, 3), near] = value[9:]
    b_d = net.send(gf.at[pl.ds(9, 3), near], g1.at[first, far], (up, j))
    g1[later, far] = value[:9]

    x_m.wait_recv()
    attended = dot(v["mxo"][...], v["w2o_v"][own_rows, :]) + dot(v["mxr"][...], v["w2o_v"][far_rows, :])
    result = v["red"][...].astype(F32) + attended.astype(BF).astype(F32)
    for h in range(2):
        v["s2o"][:, pl.ds(3 * h, 3)] = result[72 * h : 72 * h + 72].reshape(6, 3, 4, 1024).astype(BF)
    o_a = net.send(v["s2o"].at[pl.ds(0, 3)], out2.at[pl.ds(3, 3)], (i, right))
    o_b = net.send(v["s2o"].at[pl.ds(3, 3)], out2.at[pl.ds(0, 3)], (up, right))

    def section_one_back(w):
        grad_blocks = dot(v["one"][...], window_rows(g1, w).astype(BF)).astype(BF)
        v["dmix"][...] = dot(grad_blocks, v["w1o_v"][...], NT).astype(BF)
        attend_back(v["trip1"].at[w], v["dmix"], v["ps1"].at[w], v["dtrip"])
        grad = dot(v["dtrip"][...], v["w1i_v"][...], NT).astype(BF)
        grad = dot(v["one_t"][...], grad)
        grad = norm_back(grad, v["nrm"][w].astype(F32), v["rs1"][w, :, :1])
        tg[pl.ds(6 * w, 6)] = (grad + window_rows(g1, w)).reshape(6, 12, 4, 512).astype(BF)

    b_a.wait_recv()
    section_one_back(1)
    t_a = net.send(tg.at[pl.ds(6, 3), far], outg.at[pl.ds(9, 3), near], (i, right))
    t_b = net.send(tg.at[pl.ds(9, 3), far], outg.at[first, near], (up, right))
    t_c = net.send(tg.at[pl.ds(9, 3), near], outg.at[first, far], (up, j))
    keep_a = net.local(tg.at[pl.ds(6, 3), near], outg.at[pl.ds(9, 3), far])
    b_b.wait_recv()
    b_c.wait_recv()
    b_d.wait_recv()
    section_one_back(0)
    t_d = net.send(tg.at[pl.ds(0, 6), far], outg.at[pl.ds(3, 6), near], (i, right))
    keep_b = net.local(tg.at[pl.ds(0, 6), near], outg.at[pl.ds(3, 6), far])
    for copy in (o_a, o_b, t_a, t_b, t_c, t_d):
        copy.wait_recv()
    keep_a.wait()
    keep_b.wait()
    for copy in net.remotes:
        copy.wait_send()


def hand_over(in2, ing, out2, outg, held2, heldg, in_sems, out_sems):
    ways = [(a.at[pl.ds(3 * k, 3)], b.at[pl.ds(3 * k, 3)], c.at[pl.ds(3 * k, 3)])
            for a, b, c, parts in ((ing, heldg, outg, 4), (in2, held2, out2, 2)) for k in range(parts)]
    loads = [pltpu.make_async_copy(a, b, in_sems.at[n]) for n, (a, b, _) in enumerate(ways)]
    stores = [pltpu.make_async_copy(b, c, out_sems.at[n]) for n, (_, b, c) in enumerate(ways)]
    for load in loads:
        load.start()
    for load, store in zip(loads, stores):
        load.wait()
        store.start()
    for store in stores:
        store.wait()


def local(tokens, cotangent, *weights, lats, lons):
    shapes = dict(SCRATCH, wmv=((lons, 2048 // lons, 1024), BF))
    constants = [jnp.asarray(a) for a in orders()]
    anywhere = pl.BlockSpec(memory_space=pl.ANY)
    out2, outg = pl.pallas_call(
        functools.partial(body, lats, lons),
        out_shape=(jax.ShapeDtypeStruct((6, 6, 4, 1024), BF), jax.ShapeDtypeStruct((12, 12, 4, 512), BF)),
        in_specs=[anywhere] * N_IN,
        out_specs=(anywhere, anywhere),
        scratch_shapes=[pltpu.VMEM(shape, kind) for shape, kind in shapes.values()]
        + [pltpu.SemaphoreType.DMA((24,)), pltpu.SemaphoreType.DMA((N_SEM,)), pltpu.SemaphoreType.DMA((N_SEM,))],
        compiler_params=pltpu.CompilerParams(
            collective_id=0, has_side_effects=True, vmem_limit_bytes=56 * 2**20
        ),
        name="swin",
    )(tokens.transpose(1, 2, 0, 3), cotangent.transpose(1, 2, 0, 3), *weights, *constants)
    out2, outg = pl.pallas_call(
        hand_over,
        out_shape=(jax.ShapeDtypeStruct((6, 6, 4, 1024), BF), jax.ShapeDtypeStruct((12, 12, 4, 512), BF)),
        in_specs=[anywhere] * 2,
        out_specs=(anywhere, anywhere),
        scratch_shapes=[
            pltpu.VMEM((6, 6, 4, 1024), BF),
            pltpu.VMEM((12, 12, 4, 512), BF),
            pltpu.SemaphoreType.DMA((6,)),
            pltpu.SemaphoreType.DMA((6,)),
        ],
        compiler_params=pltpu.CompilerParams(vmem_limit_bytes=56 * 2**20),
        name="hand",
    )(out2, outg)
    return out2.transpose(2, 0, 1, 3), outg.transpose(2, 0, 1, 3)


def solution(mesh):
    tiles = P(None, "lat", "lon", None)
    return jax.shard_map(
        functools.partial(local, lats=mesh.shape["lat"], lons=mesh.shape["lon"]),
        mesh=mesh,
        in_specs=(tiles, tiles, P(), P(), P("lon", None), P(), P()),
        out_specs=(tiles, tiles),
        check_vma=False,
    )
```

```python
import functools

import jax
import jax.numpy as jnp
import numpy as np
from jax import lax
from jax.experimental import pallas as pl
from jax.experimental.pallas import tpu as pltpu
from jax.sharding import PartitionSpec as P

F32 = jnp.float32
BF = jnp.bfloat16
NT = ((1,), (1,))
TN = ((0,), (0,))
EPS = 1e-05
MESH = pl.DeviceIdType.MESH


def dot(a, b, dims=((1,), (0,))):
    return lax.dot_general(a, b, (dims, ((), ())), preferred_element_type=F32)


def window_place(level, row_half, counters):
    key = ("a", row_half) if level in (1, 2) else (level, row_half)
    start = {("a", 0): 0, ("a", 1): 72, (3, 0): 144, (3, 1): 180, (0, 0): 216, (0, 1): 252}[key]
    taken = counters.get(key, 0)
    counters[key] = taken + 1
    return start + taken


@functools.lru_cache(None)
def orders():
    one = np.zeros((288, 288), np.float32)
    counters = {}
    for row in range(6):
        for col in range(12):
            for lev in range(4):
                one[window_place(lev, row // 3, counters), row * 48 + col * 4 + lev] = 1
    two = np.zeros((288, 288), np.float32)
    counters = {}
    for m in range(2):
        for h in range(2):
            for row in range(6):
                for col in range(3):
                    for lev in range(4):
                        two[window_place(lev, row // 3, counters), m * 144 + h * 72 + row * 12 + col * 4 + lev] = 1
    merge = np.zeros((288, 288), np.float32)
    for p in range(2):
        for q in range(2):
            for row in range(6):
                for col in range(3):
                    for lev in range(4):
                        source = (2 * row + p) * 24 + (2 * col + q) * 4 + lev
                        merge[(p * 2 + q) * 72 + row * 12 + col * 4 + lev, source] = 1
    return tuple(np.asarray(m, dtype=BF) for m in (one, one.T, two, two.T, merge, merge.T))


def head_rows():
    lane = lax.broadcasted_iota(jnp.int32, (1, 256), 1)
    return [jnp.where((lane >= 64 * h) & (lane < 64 * h + 64), 1.0, 0.0).astype(BF) for h in range(4)]


def stack(x, rows):
    pad = jnp.zeros((16, 256), BF)
    parts = []
    for r in rows:
        parts += [x * r, pad]
    return jnp.concatenate(parts, axis=0)


def unstack(y):
    lane = lax.broadcasted_iota(jnp.int32, (144, 256), 1)
    out = y[480:624]
    for h in (2, 1, 0):
        out = jnp.where(lane < 64 * h + 64, y[160 * h : 160 * h + 144], out)
    return out


def attend(trip, mask, mixed, shares):
    rows = head_rows()
    for s in range(2):
        for g in range(2):
            r = pl.ds(144 * s, 144)
            q = trip[r, pl.ds(256 * g, 256)] * jnp.asarray(0.125, BF)
            k = trip[r, pl.ds(512 + 256 * g, 256)]
            v = trip[r, pl.ds(1024 + 256 * g, 256)]
            raised = jnp.exp(dot(k, stack(q, rows), NT) + mask[s])
            p = (raised * (1.0 / jnp.sum(raised, axis=0, keepdims=True))).astype(BF)
            shares[2 * s + g] = p
            mixed[r, pl.ds(256 * g, 256)] = unstack(dot(p, v, TN)).astype(BF)


def attend_back(trip, grad_mixed, shares, grad_trip):
    rows = head_rows()
    for s in range(2):
        for g in range(2):
            r = pl.ds(144 * s, 144)
            q = trip[r, pl.ds(256 * g, 256)] * jnp.asarray(0.125, BF)
            k = trip[r, pl.ds(512 + 256 * g, 256)]
            v = trip[r, pl.ds(1024 + 256 * g, 256)]
            do = stack(grad_mixed[r, pl.ds(256 * g, 256)], rows)
            p = shares[2 * s + g]
            wide = p.astype(F32)
            t = wide * dot(v, do, NT)
            ds = (t - wide * jnp.sum(t, axis=0, keepdims=True)).astype(BF)
            grad_trip[r, pl.ds(1024 + 256 * g, 256)] = dot(p, do).astype(BF)
            grad_trip[r, pl.ds(512 + 256 * g, 256)] = dot(ds, stack(q, rows)).astype(BF)
            grad_trip[r, pl.ds(256 * g, 256)] = (unstack(dot(ds, k, TN)) * 0.125).astype(BF)


def norm(x):
    center = x - jnp.mean(x, axis=-1, keepdims=True)
    scale = lax.rsqrt(jnp.mean(center * center, axis=-1, keepdims=True) + EPS)
    return center * scale, scale


def norm_back(grad, hat, scale):
    first = jnp.mean(grad, axis=-1, keepdims=True)
    second = jnp.mean(grad * hat, axis=-1, keepdims=True)
    return scale * (grad - first - hat * second)


SCRATCH = dict(
    tk=((12, 12, 4, 512), BF),
    nrm=((2, 288, 512), BF),
    rs1=((2, 288, 128), F32),
    trip1=((2, 288, 1536), BF),
    ps1=((2, 4, 144, 640), BF),
    mix=((288, 512), BF),
    mk=((2, 2, 144, 640), F32),
    fo=((12, 12, 4, 512), BF),
    ly=((12, 12, 4, 512), BF),
    mf=((144, 2048), F32),
    mn=((144, 2048), BF),
    rsm=((144, 128), F32),
    red=((144, 1024), BF),
    nt=((2, 144, 1024), BF),
    rs2=((144, 128), F32),
    w1i_v=((512, 1536), BF),
    w1o_v=((512, 512), BF),
    wmv=((16, 128, 1024), BF),
    w2i_v=((1024, 1536), BF),
    w2o_v=((1024, 1024), BF),
    one=((288, 288), BF),
    one_t=((288, 288), BF),
    two=((288, 288), BF),
    two_t=((288, 288), BF),
    mer=((288, 288), BF),
    mer_t=((288, 288), BF),
    cot_r=((6, 6, 4, 1024), BF),
    cot2=((2, 144, 1024), BF),
    trip2=((288, 1536), BF),
    ps2=((4, 144, 640), BF),
    mix2=((288, 512), BF),
    mxo=((144, 512), BF),
    mxs=((144, 512), BF),
    mxr=((144, 512), BF),
    dmix=((288, 512), BF),
    dmix2=((288, 512), BF),
    dtrip=((288, 1536), BF),
    pgs=((144, 1024), BF),
    pgr=((144, 1024), BF),
    pgo=((144, 1024), F32),
    gr=((144, 1024), BF),
    gmn=((144, 2048), BF),
    gf=((12, 12, 4, 512), BF),
    g1=((12, 12, 4, 512), BF),
    tg=((12, 12, 4, 512), BF),
    s2o=((6, 6, 4, 1024), BF),
)
N_IN = 13
N_SEM = 80


class Remote:
    def __init__(self, copy, when):
        self.copy, self.when = copy, when

    def run(self, act, when):
        if when is None:
            act()
        else:
            pl.when(when)(act)

    def start(self):
        self.run(self.copy.start, self.when)

    def wait_send(self):
        self.run(self.copy.wait_send, self.when)

    def wait_recv(self, when=None):
        self.run(self.copy.wait_recv, self.when if when is None else when)


class Copies:
    def __init__(self, local, send, recv):
        self.local_sems, self.send_sems, self.recv_sems = local, send, recv
        self.locals, self.remotes = 0, []

    def local(self, source, target):
        copy = pltpu.make_async_copy(source, target, self.local_sems.at[self.locals])
        self.locals += 1
        copy.start()
        return copy

    def send(self, source, target, device, when=None):
        place = len(self.remotes)
        copy = pltpu.make_async_remote_copy(
            src_ref=source,
            dst_ref=target,
            send_sem=self.send_sems.at[place],
            recv_sem=self.recv_sems.at[place],
            device_id=device,
            device_id_type=MESH,
        )
        remote = Remote(copy, when)
        remote.start()
        self.remotes.append(remote)
        return remote


class Gather:
    def __init__(self, net, wm, wmv, i, j, lats):
        self.net, self.wmv, self.i = net, wmv, i
        x_hi = j // 8
        y2 = j - x_hi * 8
        self.odd = lax.rem(i // 2, 2)
        across = i + 1 - 2 * lax.rem(i, 2)

        def same(k):
            return x_hi * 8 + lax.rem(y2 + 2 * k + 8, 8)

        def other(k):
            return (1 - x_hi) * 8 + lax.rem(y2 + 2 * k + 8, 8)

        def pick(when_odd, when_even):
            return when_odd * self.odd + when_even * (1 - self.odd)

        self.mate = (i, j + 1 - 2 * lax.rem(j, 2))
        self.z_up, self.z_down = (lax.rem(i + 2, lats), j), (lax.rem(i + lats - 2, lats), j)
        self.targets = {
            0: (pick(i, across), pick(same(-1), other(-1))),
            1: (pick(i, across), pick(same(1), other(1))),
            3: (across, other(0)),
        }
        self.onward = (i, same(1))
        self.mine = [pick(same(1), other(1)), pick(same(-1), other(-1)), pick(same(2), other(2)), other(0)]
        self.theirs = [pick(other(1), same(1)), pick(other(-1), same(-1)), pick(other(2), same(2)), other(0)]
        self.partners = [self.z_up, self.z_down, (across, other(0))]
        for step in (-1, 1):
            self.partners += [(i, same(step)), (across, other(step))]
        self.direct, self.from_z, self.to_mate = {}, {}, []
        self.wm, self.j = wm, j

    def part(self, block, row, rows):
        return self.wmv.at[block, pl.ds(row, rows)]

    def when(self, slot, value):
        return None if slot < 3 else self.odd == value

    def start(self):
        for half in range(2):
            rows = pl.ds(64 * half, 64)
            for slot in (1, 3, 0):
                self.direct[slot, half] = self.net.send(
                    self.wm.at[rows], self.wmv.at[self.j, rows], self.targets[slot], when=self.when(slot, 1)
                )
        self.to_mate.append(self.net.send(self.wm, self.wmv.at[self.j], self.mate))

    def forward(self, slot, half):
        self.direct[slot, half].wait_recv()
        block, when = self.mine[slot], self.when(slot, 1)
        whole = self.part(block, 64 * half, 64)
        if slot == 1:
            self.direct[2, half] = self.net.send(whole, whole, self.onward)
        low, high = self.part(block, 64 * half, 32), self.part(block, 64 * half + 32, 32)
        self.from_z[slot, half] = (
            self.net.send(low, low, self.z_up, when=when),
            self.net.send(high, high, self.z_down, when=when),
        )
        if slot < 3:
            self.to_mate.append(self.net.send(whole, whole, self.mate))

    def swapped(self, slot, half):
        for copy in self.from_z[slot, half]:
            copy.wait_recv(self.when(slot, 0))
        whole = self.part(self.theirs[slot], 64 * half, 64)
        self.to_mate.append(self.net.send(whole, whole, self.mate))

    def finish(self):
        for copy in self.to_mate:
            copy.wait_recv()


def body(lats, lons, *refs):
    (tok_in, cot_in, w1i, w1o, wm, w2i, w2o, c1, c1t, c2, c2t, c3, c3t) = refs[:N_IN]
    out2, outg = refs[N_IN : N_IN + 2]
    rest = refs[N_IN + 2 :]
    v = dict(zip(SCRATCH, rest))
    net = Copies(*rest[len(SCRATCH) :])
    tk, fo, ly, g1, gf, tg, wmv = (v[n] for n in ("tk", "fo", "ly", "g1", "gf", "tg", "wmv"))

    i, j = lax.axis_index("lat"), lax.axis_index("lon")
    up, down = lax.rem(i + 1, lats), lax.rem(i + lats - 1, lats)
    right, left = lax.rem(j + 1, lons), lax.rem(j + lons - 1, lons)
    core = lax.rem(j, 2)
    mate = j + 1 - 2 * core
    ring = lons == 16
    partners = [(i, right), (i, left), (up, j), (down, j), (up, right), (down, left)]
    gather = Gather(net, wm, wmv, i, j, lats) if ring else None
    partners += gather.partners if ring else [(i, lax.rem(j + d, lons)) for d in range(1, lons)]

    barrier = pltpu.get_barrier_semaphore()
    for device in partners:
        pl.semaphore_signal(barrier, inc=1, device_id=device, device_id_type=MESH)

    first, later, near, far = pl.ds(0, 3), pl.ds(3, 9), pl.ds(0, 6), pl.ds(6, 6)
    in_tok = net.local(tok_in.at[later, far], tk.at[pl.ds(0, 9), near])
    in_one = net.local(c1, v["one"])
    in_w1i = net.local(w1i, v["w1i_v"])
    in_w1o = net.local(w1o, v["w1o_v"])
    in_one_t = net.local(c1t, v["one_t"])
    in_wm = net.local(wm, wmv.at[j])
    in_rest = [net.local(a, v[n]) for a, n in ((c3, "mer"), (c2, "two"))]
    in_w2i = [
        net.local(
            w2i.at[:, pl.ds(pl.multiple_of(1024 * part + 512 * core, 512), 512)],
            v["w2i_v"].at[:, pl.ds(512 * part, 512)],
        )
        for part in range(3)
    ]
    in_w2o = net.local(w2o, v["w2o_v"])
    in_late = [net.local(a, v[n]) for a, n in ((c2t, "two_t"), (c3t, "mer_t"))]

    pl.semaphore_wait(barrier, len(partners))

    r_a = net.send(tok_in.at[pl.ds(3, 6), near], tk.at[pl.ds(0, 6), far], (i, left))
    r_b = net.send(tok_in.at[pl.ds(9, 3), near], tk.at[pl.ds(6, 3), far], (i, left))
    r_c = net.send(tok_in.at[first, far], tk.at[pl.ds(9, 3), near], (down, j))
    r_d = net.send(tok_in.at[first, near], tk.at[pl.ds(9, 3), far], (down, left))

    depth = wm.shape[0]
    everywhere = []
    if ring:
        gather.start()
    else:
        for d in range(1, lons):
            everywhere.append(net.send(wm, wmv.at[j], (i, lax.rem(j + d, lons))))

    def merge_rows(b):
        if depth <= 256:
            count = 256 // depth
            return wmv[pl.ds(count * b, count)].reshape(256, 1024)
        return wmv[256 * b // depth, pl.ds(256 * b % depth, 256)]

    lane = lax.broadcasted_iota(jnp.int32, (1, 640), 1)
    lane = lane - 160 * (
        (lane >= 160).astype(jnp.int32) + (lane >= 320).astype(jnp.int32) + (lane >= 480).astype(jnp.int32)
    )
    key = lax.broadcasted_iota(jnp.int32, (144, 1), 0)

    def quarter(index):
        return (index >= 36).astype(jnp.int32) + (index >= 72).astype(jnp.int32) + (index >= 108).astype(jnp.int32)

    pad = lane >= 144
    half_mask = jnp.where(((key >= 72) == (lane >= 72)) | pad, 0.0, -1e30)
    quarter_mask = jnp.where((quarter(key) == quarter(lane)) | pad, 0.0, -1e30)
    last = jnp.broadcast_to(i, (144, 640)) == lats - 1
    v["mk"][0, 0] = jnp.zeros((144, 640), F32)
    v["mk"][0, 1] = half_mask
    v["mk"][1, 0] = jnp.where(last, half_mask, 0.0)
    v["mk"][1, 1] = jnp.where(last, quarter_mask, half_mask)

    def window_rows(ref, w):
        return ref[pl.ds(6 * w, 6)].astype(F32).reshape(288, 512)

    def section_one(w, between):
        hat, scale = norm(window_rows(tk, w))
        normed = hat.astype(BF)
        v["nrm"][w] = normed
        v["rs1"][w] = jnp.broadcast_to(scale, (288, 128))
        blocks = dot(v["one"][...], normed).astype(BF)
        for n in range(0, 1536, 256):
            v["trip1"][w, :, pl.ds(n, 256)] = dot(blocks, v["w1i_v"][:, pl.ds(n, 256)]).astype(BF)
        pump(between)
        attend(v["trip1"].at[w], v["mk"].at[w], v["mix"], v["ps1"].at[w])
        projected = dot(v["mix"][...], v["w1o_v"][...]).astype(BF)
        value = window_rows(tk, w) + dot(v["one_t"][...], projected)
        fo[pl.ds(6 * w, 6)] = value.reshape(6, 12, 4, 512).astype(BF)

    def pump(steps):
        if ring:
            for act, slot, half in steps:
                getattr(gather, act)(slot, half)

    in_one.wait()
    in_w1i.wait()
    in_w1o.wait()
    in_one_t.wait()
    in_tok.wait()
    r_a.wait_recv()
    pump([("forward", 1, 0)])
    section_one(0, [("forward", 3, 0)])
    f_a = net.send(fo.at[pl.ds(3, 3), near], ly.at[pl.ds(0, 3), far], (i, left))
    f_b = net.send(fo.at[first, near], ly.at[pl.ds(9, 3), far], (down, left))
    f_c = net.send(fo.at[first, far], ly.at[pl.ds(9, 3), near], (down, j))
    pump([("forward", 0, 0), ("forward", 1, 1)])
    r_b.wait_recv()
    r_c.wait_recv()
    r_d.wait_recv()
    section_one(1, [("forward", 2, 0), ("forward", 3, 1)])
    f_d = net.send(fo.at[pl.ds(6, 6), near], ly.at[pl.ds(3, 6), far], (i, left))
    ly[pl.ds(0, 9), near] = fo[later, far]
    pump([("forward", 0, 1), ("swapped", 1, 0), ("swapped", 3, 0), ("swapped", 0, 0), ("forward", 2, 1)])
    cot_a = net.send(cot_in.at[pl.ds(3, 3)], v["cot_r"].at[pl.ds(0, 3)], (i, left))
    cot_b = net.send(cot_in.at[pl.ds(0, 3)], v["cot_r"].at[pl.ds(3, 3)], (down, left))
    for copy in in_rest:
        copy.wait()

    def merge_half(h):
        value = dot(v["mer"][...], ly[:, pl.ds(6 * h, 6)].astype(F32).reshape(288, 512).astype(BF))
        for pq in range(4):
            v["mf"][pl.ds(72 * h, 72), pl.ds(512 * pq, 512)] = value[72 * pq : 72 * pq + 72]

    f_c.wait_recv()
    merge_half(0)
    f_a.wait_recv()
    f_b.wait_recv()
    f_d.wait_recv()
    merge_half(1)
    pump([("swapped", 2, 0), ("swapped", 1, 1), ("swapped", 3, 1), ("swapped", 0, 1)])
    hat, scale = norm(v["mf"][...])
    v["mn"][...] = hat.astype(BF)
    v["rsm"][...] = jnp.broadcast_to(scale, (144, 128))
    pump([("swapped", 2, 1)])

    cot_a.wait_recv()
    cot_b.wait_recv()
    halves = [v["cot_r"][:, pl.ds(3 * h, 3)].astype(F32).reshape(72, 1024) for h in range(2)]
    v["cot2"][0] = jnp.concatenate(halves, axis=0).astype(BF)
    cot_m = net.send(v["cot2"].at[0], v["cot2"].at[1], (i, mate))

    in_wm.wait()
    if ring:
        gather.finish()
    for copy in everywhere:
        copy.wait_recv()
    merged = v["mn"][...]
    for n in range(0, 1024, 256):
        v["red"][:, pl.ds(n, 256)] = dot(merged, wmv[:, :, pl.ds(n, 256)].reshape(2048, 256)).astype(BF)
    hat, scale = norm(v["red"][...].astype(F32))
    v["nt"][0] = hat.astype(BF)
    v["rs2"][...] = jnp.broadcast_to(scale, (144, 128))
    n_m = net.send(v["nt"].at[0], v["nt"].at[1], (i, mate))

    own_rows = pl.ds(pl.multiple_of(512 * core, 512), 512)
    far_rows = pl.ds(pl.multiple_of(512 - 512 * core, 512), 512)
    in_w2o.wait()
    cot_m.wait_recv()
    grad_blocks = dot(v["two"][...], v["cot2"][...].reshape(288, 1024)).astype(BF)
    v["dmix2"][...] = dot(grad_blocks, v["w2o_v"][own_rows, :], NT).astype(BF)
    for copy in in_w2i + in_late:
        copy.wait()

    def project_two(m):
        for n in range(0, 1536, 256):
            part = dot(v["nt"][m], v["w2i_v"][:, pl.ds(n, 256)]).astype(BF)
            v["dtrip"][pl.ds(144 * m, 144), pl.ds(n, 256)] = part

    project_two(0)
    n_m.wait_recv()
    project_two(1)
    for n in range(0, 1536, 256):
        v["trip2"][:, pl.ds(n, 256)] = dot(v["two"][...], v["dtrip"][:, pl.ds(n, 256)]).astype(BF)
    attend(v["trip2"], v["mk"].at[1], v["mix2"], v["ps2"])
    mixed = dot(v["two_t"][...], v["mix2"][...]).astype(BF)
    v["mxo"][...] = mixed[:144]
    v["mxs"][...] = mixed[144:]
    x_m = net.send(v["mxs"], v["mxr"], (i, mate))

    attend_back(v["trip2"], v["dmix2"], v["ps2"], v["dtrip"])
    back = dot(v["two_t"][...], v["dtrip"][...]).astype(BF)
    for n in range(0, 1024, 256):
        v["pgs"][:, pl.ds(n, 256)] = dot(back[144:], v["w2i_v"][pl.ds(n, 256), :], NT).astype(BF)
    p_m = net.send(v["pgs"], v["pgr"], (i, mate))
    for n in range(0, 1024, 256):
        v["pgo"][:, pl.ds(n, 256)] = dot(back[:144], v["w2i_v"][pl.ds(n, 256), :], NT)
    p_m.wait_recv()
    grad = (v["pgo"][...] + v["pgr"][...].astype(F32)).astype(BF).astype(F32)
    grad = norm_back(grad, v["nt"][0].astype(F32), v["rs2"][:, :1])
    v["gr"][...] = (grad + v["cot2"][0].astype(F32)).astype(BF)
    for b in range(8):
        rows = merge_rows(b)
        v["gmn"][:, pl.ds(256 * b, 256)] = dot(v["gr"][...], rows, NT).astype(BF)
    v["mf"][...] = norm_back(v["gmn"][...].astype(F32), v["mn"][...].astype(F32), v["rsm"][:, :1])

    def unmerge_half(h):
        rows = v["mf"][pl.ds(72 * h, 72), :]
        value = jnp.concatenate([rows[:, 512 * pq : 512 * pq + 512] for pq in range(4)], axis=0).astype(BF)
        return dot(v["mer_t"][...], value).reshape(12, 6, 4, 512).astype(BF)

    gf[:, far] = unmerge_half(1)
    b_a = net.send(gf.at[pl.ds(3, 6), far], g1.at[pl.ds(6, 6), near], (i, right))
    b_b = net.send(gf.at[first, far], g1.at[pl.ds(3, 3), near], (i, right))
    b_c = net.send(gf.at[pl.ds(9, 3), far], g1.at[first, near], (up, right))
    value = unmerge_half(0)
    gf[pl.ds(9, 3), near] = value[9:]
    b_d = net.send(gf.at[pl.ds(9, 3), near], g1.at[first, far], (up, j))
    g1[later, far] = value[:9]

    x_m.wait_recv()
    attended = dot(v["mxo"][...], v["w2o_v"][own_rows, :]) + dot(v["mxr"][...], v["w2o_v"][far_rows, :])
    result = v["red"][...].astype(F32) + attended.astype(BF).astype(F32)
    for h in range(2):
        v["s2o"][:, pl.ds(3 * h, 3)] = result[72 * h : 72 * h + 72].reshape(6, 3, 4, 1024).astype(BF)
    o_a = net.send(v["s2o"].at[pl.ds(0, 3)], out2.at[pl.ds(3, 3)], (i, right))
    o_b = net.send(v["s2o"].at[pl.ds(3, 3)], out2.at[pl.ds(0, 3)], (up, right))

    def section_one_back(w):
        grad_blocks = dot(v["one"][...], window_rows(g1, w).astype(BF)).astype(BF)
        v["dmix"][...] = dot(grad_blocks, v["w1o_v"][...], NT).astype(BF)
        attend_back(v["trip1"].at[w], v["dmix"], v["ps1"].at[w], v["dtrip"])
        grad = dot(v["dtrip"][...], v["w1i_v"][...], NT).astype(BF)
        grad = dot(v["one_t"][...], grad)
        grad = norm_back(grad, v["nrm"][w].astype(F32), v["rs1"][w, :, :1])
        tg[pl.ds(6 * w, 6)] = (grad + window_rows(g1, w)).reshape(6, 12, 4, 512).astype(BF)

    b_a.wait_recv()
    section_one_back(1)
    t_a = net.send(tg.at[pl.ds(6, 3), far], outg.at[pl.ds(9, 3), near], (i, right))
    t_b = net.send(tg.at[pl.ds(9, 3), far], outg.at[first, near], (up, right))
    t_c = net.send(tg.at[pl.ds(9, 3), near], outg.at[first, far], (up, j))
    keep_a = net.local(tg.at[pl.ds(6, 3), near], outg.at[pl.ds(9, 3), far])
    b_b.wait_recv()
    b_c.wait_recv()
    b_d.wait_recv()
    section_one_back(0)
    t_d = net.send(tg.at[pl.ds(0, 6), far], outg.at[pl.ds(3, 6), near], (i, right))
    keep_b = net.local(tg.at[pl.ds(0, 6), near], outg.at[pl.ds(3, 6), far])
    for copy in (o_a, o_b, t_a, t_b, t_c, t_d):
        copy.wait_recv()
    keep_a.wait()
    keep_b.wait()
    for copy in net.remotes:
        copy.wait_send()


def hand_over(in2, ing, out2, outg, held2, heldg, in_sems, out_sems):
    ways = [(a.at[pl.ds(3 * k, 3)], b.at[pl.ds(3 * k, 3)], c.at[pl.ds(3 * k, 3)])
            for a, b, c, parts in ((ing, heldg, outg, 4), (in2, held2, out2, 2)) for k in range(parts)]
    loads = [pltpu.make_async_copy(a, b, in_sems.at[n]) for n, (a, b, _) in enumerate(ways)]
    stores = [pltpu.make_async_copy(b, c, out_sems.at[n]) for n, (_, b, c) in enumerate(ways)]
    for load in loads:
        load.start()
    for load, store in zip(loads, stores):
        load.wait()
        store.start()
    for store in stores:
        store.wait()


def local(tokens, cotangent, *weights, lats, lons):
    shapes = dict(SCRATCH, wmv=((lons, 2048 // lons, 1024), BF))
    constants = [jnp.asarray(a) for a in orders()]
    anywhere = pl.BlockSpec(memory_space=pl.ANY)
    out2, outg = pl.pallas_call(
        functools.partial(body, lats, lons),
        out_shape=(jax.ShapeDtypeStruct((6, 6, 4, 1024), BF), jax.ShapeDtypeStruct((12, 12, 4, 512), BF)),
        in_specs=[anywhere] * N_IN,
        out_specs=(anywhere, anywhere),
        scratch_shapes=[pltpu.VMEM(shape, kind) for shape, kind in shapes.values()]
        + [pltpu.SemaphoreType.DMA((24,)), pltpu.SemaphoreType.DMA((N_SEM,)), pltpu.SemaphoreType.DMA((N_SEM,))],
        compiler_params=pltpu.CompilerParams(
            collective_id=0, has_side_effects=True, vmem_limit_bytes=56 * 2**20
        ),
        name="swin",
    )(tokens.transpose(1, 2, 0, 3), cotangent.transpose(1, 2, 0, 3), *weights, *constants)
    out2, outg = pl.pallas_call(
        hand_over,
        out_shape=(jax.ShapeDtypeStruct((6, 6, 4, 1024), BF), jax.ShapeDtypeStruct((12, 12, 4, 512), BF)),
        in_specs=[anywhere] * 2,
        out_specs=(anywhere, anywhere),
        scratch_shapes=[
            pltpu.VMEM((6, 6, 4, 1024), BF),
            pltpu.VMEM((12, 12, 4, 512), BF),
            pltpu.SemaphoreType.DMA((6,)),
            pltpu.SemaphoreType.DMA((6,)),
        ],
        compiler_params=pltpu.CompilerParams(vmem_limit_bytes=56 * 2**20),
        name="hand",
    )(out2, outg)
    return out2.transpose(2, 0, 1, 3), outg.transpose(2, 0, 1, 3)


def solution(mesh):
    tiles = P(None, "lat", "lon", None)
    return jax.shard_map(
        functools.partial(local, lats=mesh.shape["lat"], lons=mesh.shape["lon"]),
        mesh=mesh,
        in_specs=(tiles, tiles, P(), P(), P("lon", None), P(), P()),
        out_specs=(tiles, tiles),
        check_vma=False,
    )
```
